512 devices in a mesh: dp: 64 (over z_lo, y, core), mp: 8 (over z_hi, x).
Axes of the slice: x: 4, y: 8, z: 8 (z_hi: 2, z_lo: 4; z = z_hi * 4 + z_lo), core: 2. Of those that a mesh axis runs over, the one named last changes fastest.
Arguments:
- tokens: bfloat16 [24576, 1024], P('dp', 'mp'), may hold values from -400 to 400
- cotangent: bfloat16 [24576, 8192], P('dp', 'mp'), may hold values from -1.5625 to 1.5625
Outputs:
- update: bfloat16 [1024, 8192], P('dp', 'mp')
The draws below stay inside these ranges and needn't reach their ends.
All inputs are finite; a program needn't handle non-finite values.
Results may differ from the reference program's by a relative error of at most 0.012.
The reference program's roundings to bfloat16 on the way count: a program that leaves them out, or rounds other values in their place, can miss the bound.
Values may be sent and summed in bfloat16 or wider, within the bound.
No kernel may reach another device: no remote copies, remote signals or barrier semaphores. Data moves between devices by JAX's collectives and lax.ppermute only.
A program may use at most 64 MiB of HBM per device.

```python
import math
import jax
import jax.numpy as jnp
from jax import lax

BLK = 512
ITERS = 4
TOKENS = 24576
DR = 1024
DC = 8192


def scaled_field(key, rows, cols, factor):
    key_values, key_rows, key_cols = jax.random.split(key, 3)
    row_scale = jnp.exp(jax.random.uniform(key_rows, (rows, 1), jnp.float32, 0.0, math.log(10.0)))
    col_scale = jnp.exp(jax.random.uniform(key_cols, (1, cols), jnp.float32, 0.0, math.log(10.0)))
    values = jnp.clip(jax.random.normal(key_values, (rows, cols), jnp.float32), -4.0, 4.0)
    return values * row_scale * col_scale * factor


def draw_tokens(key, part):
    key = jax.random.fold_in(key, 11)
    return scaled_field(key, TOKENS, DR, 1.0).astype(jnp.bfloat16)


def draw_cotangent(key, part):
    key = jax.random.fold_in(key, 23)
    return scaled_field(key, TOKENS, DC, 0.00390625).astype(jnp.bfloat16)


def setup_inputs(seed: int = 0) -> dict:
    splits = jax.random.split(jax.random.key(seed), 3)
    tokens = draw_tokens(jax.random.fold_in(splits[2], 71), 0)
    cotangent = draw_cotangent(jax.random.fold_in(splits[2], 71), 0)
    return dict(tokens=tokens, cotangent=cotangent)


def root_of(gram):
    size = gram.shape[0]
    identity = jnp.eye(size, dtype=jnp.float32)
    damp = 0.1 * jnp.trace(gram) / size + 1e-06
    matrix = gram + damp * identity
    frobenius = jnp.sqrt(jnp.sum(matrix * matrix))
    current = matrix / frobenius
    estimate = frobenius ** (-0.25) * identity
    for _ in range(ITERS):
        factor = ((5.0 * identity - current) * 0.25).astype(jnp.bfloat16)
        square = jnp.dot(factor, factor, preferred_element_type=jnp.float32).astype(jnp.bfloat16)
        fourth = jnp.dot(square, square, preferred_element_type=jnp.float32).astype(jnp.bfloat16)
        current = jnp.dot(fourth, current.astype(jnp.bfloat16), preferred_element_type=jnp.float32)
        estimate = jnp.dot(estimate.astype(jnp.bfloat16), factor, preferred_element_type=jnp.float32)
    return estimate.astype(jnp.bfloat16)

def left_root(block):
    return root_of(jnp.dot(block, block.T, preferred_element_type=jnp.float32))

def right_root(block):
    return root_of(jnp.dot(block.T, block, preferred_element_type=jnp.float32))

def apply_roots(triple):
    lroot, block, rroot = triple
    half = jnp.dot(lroot, block, preferred_element_type=jnp.float32).astype(jnp.bfloat16)
    return jnp.dot(half, rroot, preferred_element_type=jnp.float32).astype(jnp.bfloat16)

def reference(tokens, cotangent):
    grad = jnp.dot(tokens.T, cotangent, preferred_element_type=jnp.float32).astype(jnp.bfloat16)
    col_blocks = DC // BLK
    blocks = grad.reshape(2, BLK, col_blocks, BLK).transpose(0, 2, 1, 3).reshape(2 * col_blocks, BLK, BLK)
    lefts = lax.map(left_root, blocks)
    rights = lax.map(right_root, blocks)
    pieces = lax.map(apply_roots, (lefts, blocks, rights))
    return pieces.reshape(2, col_blocks, BLK, BLK).transpose(0, 2, 1, 3).reshape(DR, DC)
```

```python
import functools

import jax
import jax.numpy as jnp
from jax import lax
from jax.experimental import pallas as pl
from jax.experimental.pallas import tpu as pltpu
from jax.sharding import Mesh
from jax.sharding import PartitionSpec as P

BLK = 512
ITERS = 4
ROWS = 32
VMEM_BYTES = 48 * 1024 * 1024


def dot(left, right, dims=((1,), (0,))):
    return lax.dot_general(left, right, (dims, ((), ())), preferred_element_type=jnp.float32)


def contract_kernel(core_ref, tokens_ref, cotangent_ref, partial_ref):
    for half in range(2):
        for place in range(4):
            total = None
            for source in range(2):
                term = dot(
                    tokens_ref[source, place, half], cotangent_ref[source], ((0,), (0,))
                )
                total = term if total is None else total + term
            row = half * BLK + place * 128
            partial_ref[row : row + 128, :] = total.astype(partial_ref.dtype)


def contract(core, tokens, cotangent):
    return pl.pallas_call(
        contract_kernel,
        grid_spec=pltpu.PrefetchScalarGridSpec(
            num_scalar_prefetch=1,
            grid=(1,),
            in_specs=[
                pl.BlockSpec(tokens.shape, lambda i, core: (0, 0, 0, 0, 0)),
                pl.BlockSpec((2, 384, BLK), lambda i, core: (0, 0, core[0])),
            ],
            out_specs=pl.BlockSpec((2 * BLK, BLK), lambda i, core: (0, 0)),
        ),
        out_shape=jax.ShapeDtypeStruct((2 * BLK, BLK), jnp.bfloat16),
        compiler_params=pltpu.CompilerParams(vmem_limit_bytes=VMEM_BYTES),
        name="contract",
    )(core, tokens, cotangent)


def roots_kernel(first_ref, block_ref, out_ref, left_ref, right_ref):
    block = block_ref[...]
    row_ids = lax.broadcasted_iota(jnp.int32, (BLK, BLK), 0)
    col_ids = lax.broadcasted_iota(jnp.int32, (BLK, BLK), 1)
    eye = jnp.where(row_ids == col_ids, 1.0, 0.0).astype(jnp.float32)

    def start(gram):
        damp = 0.1 * jnp.sum(gram * eye) / BLK + 1e-06
        matrix = gram + damp * eye
        fro = jnp.sqrt(jnp.sum(matrix * matrix, keepdims=True))
        return matrix / fro, jnp.sqrt(jnp.sqrt(1.0 / fro))

    left, left_scale = start(dot(block, block, ((1,), (1,))))
    right, right_scale = start(dot(block, block, ((0,), (0,))))
    scales = (left_scale, right_scale)
    first = first_ref[0]
    pick_row = lax.broadcasted_iota(jnp.int32, (ROWS, BLK), 0) + first
    pick_col = lax.broadcasted_iota(jnp.int32, (ROWS, BLK), 1)
    rows = jnp.where(pick_row == pick_col, left_scale, 0.0)
    steps = []
    for it in range(ITERS):
        factors = [((5.0 * eye - m) * 0.25).astype(jnp.bfloat16) for m in (left, right)]
        rows = dot(rows.astype(jnp.bfloat16), factors[0])
        steps.append(factors[1])
        if it < ITERS - 1:
            squares = [dot(f, f).astype(jnp.bfloat16) for f in factors]
            fourths = [dot(s, s).astype(jnp.bfloat16) for s in squares]
            left, right = (
                dot(f, m.astype(jnp.bfloat16)) for f, m in zip(fourths, (left, right))
            )
    half = dot(rows.astype(jnp.bfloat16), block).astype(jnp.bfloat16)
    value = half * right_scale.astype(jnp.bfloat16)
    for it in range(ITERS):
        value = dot(value.astype(jnp.bfloat16), steps[it])
    out_ref[...] = value.astype(out_ref.dtype)


def apply_roots(first, block):
    return pl.pallas_call(
        roots_kernel,
        in_specs=[
            pl.BlockSpec(memory_space=pltpu.SMEM),
            pl.BlockSpec(memory_space=pltpu.VMEM),
        ],
        out_specs=pl.BlockSpec(memory_space=pltpu.VMEM),
        out_shape=jax.ShapeDtypeStruct((ROWS, BLK), jnp.bfloat16),
        scratch_shapes=[pltpu.VMEM((8, 128), jnp.float32)] * 2,
        compiler_params=pltpu.CompilerParams(vmem_limit_bytes=VMEM_BYTES),
        name="apply_roots",
    )(first, block)


def body(tokens, cotangent):
    core = lax.axis_index("core")
    features = lax.all_gather(tokens[None], "zh", axis=0, tiled=True)
    features = lax.all_gather(features[None], "x", axis=0, tiled=True)
    features = lax.all_gather(features[None], "core", axis=0, tiled=True)
    both = lax.all_gather(cotangent[None], "core", axis=0, tiled=True)
    partial = contract(core[None], features, both)
    shares = lax.all_to_all(
        partial.reshape(32, ROWS, BLK), ("zr", "zp", "y"), 0, 0, tiled=True
    )
    own_rows = jnp.sum(shares.astype(jnp.float32), axis=0).astype(jnp.bfloat16)
    block = lax.all_gather(own_rows, "zp", axis=0, tiled=True)
    block = lax.all_gather(block, "y", axis=0, tiled=True)
    first = (lax.axis_index("y") * 2 + lax.axis_index("zp")) * ROWS
    update = apply_roots(first[None], block)
    pieces = lax.all_to_all(update.reshape(2, 16, BLK), "core", 0, 0, tiled=True)
    return jnp.concatenate([pieces[0], pieces[1]], axis=1)


def solution(mesh):
    devices = mesh.devices.reshape(2, 2, 8, 2, 2, 4)
    fine = Mesh(devices, ("zr", "zp", "y", "core", "zh", "x"))
    spec = P(("zr", "zp", "y", "core"), ("zh", "x"))
    return jax.shard_map(
        body, mesh=fine, in_specs=(spec, spec), out_specs=spec, check_vma=False
    )
```

```python
import jax
import jax.numpy as jnp
from jax import lax
from jax.experimental import pallas as pl
from jax.experimental.pallas import tpu as pltpu
from jax.sharding import Mesh
from jax.sharding import PartitionSpec as P

BLK = 512
ITERS = 4
ROWS = 32
VMEM_BYTES = 48 * 1024 * 1024
VMEM_SPEC = pl.BlockSpec(memory_space=pltpu.VMEM)


def dot(left, right, dims=((1,), (0,))):
    return lax.dot_general(left, right, (dims, ((), ())), preferred_element_type=jnp.float32)


def own_kernel(tokens_ref, cotangent_ref, partial_ref):
    for place in range(8):
        partial_ref[place * 128 : place * 128 + 128, :] = dot(
            tokens_ref[place], cotangent_ref[...], ((0,), (0,))
        )


def pair_kernel(parity_ref, tokens_ref, cotangent_ref, own_ref, keep_ref, low_ref, high_ref, total_ref):
    parity = parity_ref[0]
    for place in range(8):
        total_ref[...] = own_ref[place * 128 : place * 128 + 128, :] + dot(
            tokens_ref[place], cotangent_ref[...], ((0,), (0,))
        )
        for group in range(2):
            row = place * 64 + group * ROWS
            kept = pl.multiple_of(group * 64 + parity * ROWS, ROWS)
            sent = pl.multiple_of(group * 64 + (1 - parity) * ROWS, ROWS)
            keep_ref[row : row + ROWS, :] = total_ref[pl.ds(kept, ROWS), :]
            other = total_ref[pl.ds(sent, ROWS), :].astype(jnp.bfloat16)
            low_ref[row : row + ROWS, :] = other[:, :256]
            high_ref[row : row + ROWS, :] = other[:, 256:]


def contract_own(tokens, cotangent):
    return pl.pallas_call(
        own_kernel,
        in_specs=[VMEM_SPEC] * 2,
        out_specs=VMEM_SPEC,
        out_shape=jax.ShapeDtypeStruct((2 * BLK, BLK), jnp.float32),
        compiler_params=pltpu.CompilerParams(vmem_limit_bytes=VMEM_BYTES),
        cost_estimate=pl.CostEstimate(flops=2 * 384 * 1024 * 512, bytes_accessed=3 << 20, transcendentals=0),
        name="contract_own",
    )(tokens, cotangent)


def contract_pair(parity, tokens, cotangent, own):
    half = jax.ShapeDtypeStruct((BLK, 256), jnp.bfloat16)
    return pl.pallas_call(
        pair_kernel,
        in_specs=[pl.BlockSpec(memory_space=pltpu.SMEM)] + [VMEM_SPEC] * 3,
        out_specs=[VMEM_SPEC] * 3,
        out_shape=[jax.ShapeDtypeStruct((BLK, BLK), jnp.float32), half, half],
        scratch_shapes=[pltpu.VMEM((128, BLK), jnp.float32)],
        compiler_params=pltpu.CompilerParams(vmem_limit_bytes=VMEM_BYTES),
        cost_estimate=pl.CostEstimate(flops=2 * 384 * 1024 * 512, bytes_accessed=5 << 20, transcendentals=0),
        name="contract_pair",
    )(parity, tokens, cotangent, own)


def add_kernel(keep_ref, low_ref, high_ref, sum_ref):
    for share in range(16):
        rows = slice(share * ROWS, share * ROWS + ROWS)
        sum_ref[share, :, :256] = (keep_ref[rows, :256] + low_ref[rows, :].astype(jnp.float32)).astype(jnp.bfloat16)
        sum_ref[share, :, 256:] = (keep_ref[rows, 256:] + high_ref[rows, :].astype(jnp.float32)).astype(jnp.bfloat16)


def add_pair(keep, low, high):
    return pl.pallas_call(
        add_kernel,
        in_specs=[VMEM_SPEC] * 3,
        out_specs=VMEM_SPEC,
        out_shape=jax.ShapeDtypeStruct((16, ROWS, BLK), jnp.bfloat16),
        compiler_params=pltpu.CompilerParams(vmem_limit_bytes=VMEM_BYTES),
        name="add_pair",
    )(keep, low, high)


def total_kernel(shares_ref, copies_ref):
    total = shares_ref[0].astype(jnp.float32)
    for share in range(1, 16):
        total += shares_ref[share].astype(jnp.float32)
    total = total.astype(jnp.bfloat16)
    for copy in range(16):
        copies_ref[copy] = total


def total_copies(shares):
    return pl.pallas_call(
        total_kernel,
        in_specs=[VMEM_SPEC],
        out_specs=VMEM_SPEC,
        out_shape=jax.ShapeDtypeStruct((16, ROWS, BLK), jnp.bfloat16),
        compiler_params=pltpu.CompilerParams(vmem_limit_bytes=VMEM_BYTES),
        name="total_copies",
    )(shares)


def roots_kernel(first_ref, block_ref, out_ref):
    block = block_ref[...]
    row_ids = lax.broadcasted_iota(jnp.int32, (BLK, BLK), 0)
    col_ids = lax.broadcasted_iota(jnp.int32, (BLK, BLK), 1)
    eye = jnp.where(row_ids == col_ids, 1.0, 0.0).astype(jnp.float32)

    def start(gram):
        damp = 0.1 * jnp.sum(gram * eye) / BLK + 1e-06
        matrix = gram + damp * eye
        fro = jnp.sqrt(jnp.sum(matrix * matrix, keepdims=True))
        return matrix / fro, jnp.sqrt(jnp.sqrt(1.0 / fro))

    left, left_scale = start(dot(block, block, ((1,), (1,))))
    right, right_scale = start(dot(block, block, ((0,), (0,))))
    first = first_ref[0]
    pick_row = lax.broadcasted_iota(jnp.int32, (ROWS, BLK), 0) + first
    pick_col = lax.broadcasted_iota(jnp.int32, (ROWS, BLK), 1)
    rows = jnp.where(pick_row == pick_col, left_scale, 0.0)
    steps = []
    for it in range(ITERS):
        factors = [((5.0 * eye - m) * 0.25).astype(jnp.bfloat16) for m in (left, right)]
        rows = dot(rows.astype(jnp.bfloat16), factors[0])
        steps.append(factors[1])
        if it < ITERS - 1:
            squares = [dot(f, f).astype(jnp.bfloat16) for f in factors]
            fourths = [dot(s, s).astype(jnp.bfloat16) for s in squares]
            left, right = (
                dot(f, m.astype(jnp.bfloat16)) for f, m in zip(fourths, (left, right))
            )
    half = dot(rows.astype(jnp.bfloat16), block).astype(jnp.bfloat16)
    value = half * right_scale.astype(jnp.bfloat16)
    for it in range(ITERS):
        value = dot(value.astype(jnp.bfloat16), steps[it])
    out_ref[...] = value.astype(out_ref.dtype)


def apply_roots(first, block):
    return pl.pallas_call(
        roots_kernel,
        in_specs=[pl.BlockSpec(memory_space=pltpu.SMEM), VMEM_SPEC],
        out_specs=VMEM_SPEC,
        out_shape=jax.ShapeDtypeStruct((ROWS, BLK), jnp.bfloat16),
        compiler_params=pltpu.CompilerParams(vmem_limit_bytes=VMEM_BYTES),
        name="apply_roots",
    )(first, block)


def swap(value, axis):
    return lax.ppermute(value, axis, [(0, 1), (1, 0)])


def neighbours(value, up):
    pairs = [(i, (i + 1 if (i % 2 == 0) == up else i - 1) % 8) for i in range(8)]
    return lax.ppermute(value, ("q", "p"), pairs)


def body(tokens, cotangent):
    core = lax.axis_index("core")
    parity = lax.axis_index("p")
    first = lax.axis_index("zp") * 256 + lax.axis_index("q") * 64 + parity * ROWS
    sent = lax.dynamic_slice_in_dim(cotangent, (1 - core) * BLK, BLK, 1)
    other_cotangent = swap(sent, "core")
    own_cotangent = lax.dynamic_slice_in_dim(cotangent, core * BLK, BLK, 1)
    copies = jnp.broadcast_to(tokens[None], (8, *tokens.shape))
    features = lax.all_to_all(copies, ("zh", "x"), 0, 0, tiled=True)
    other_features = swap(features, "core")
    own = contract_own(features, own_cotangent)
    keep, low, high = contract_pair(parity[None], other_features, other_cotangent, own)
    shares = add_pair(keep, neighbours(low, True), neighbours(high, False))
    shares = lax.all_to_all(shares, ("zr", "zp", "q"), 0, 0, tiled=True)
    rows = lax.all_to_all(total_copies(shares), ("zp", "q", "p"), 0, 0, tiled=True)
    update = apply_roots(first[None], rows.reshape(BLK, BLK))
    return lax.all_to_all(update, "core", split_axis=0, concat_axis=1, tiled=True)


def solution(mesh):
    devices = mesh.devices.reshape(2, 2, 4, 2, 2, 2, 4)
    fine = Mesh(devices, ("zr", "zp", "q", "p", "core", "zh", "x"))
    spec = P(("zr", "zp", "q", "p", "core"), ("zh", "x"))
    return jax.shard_map(
        body, mesh=fine, in_specs=(spec, spec), out_specs=spec, check_vma=False
    )
```

```python
import jax
import jax.numpy as jnp
from jax import lax
from jax.experimental import pallas as pl
from jax.experimental.pallas import tpu as pltpu
from jax.sharding import Mesh
from jax.sharding import PartitionSpec as P

BLK = 512
ITERS = 4
ROWS = 32
PARAMS = pltpu.CompilerParams(vmem_limit_bytes=48 * 1024 * 1024)
VMEM = pl.BlockSpec(memory_space=pltpu.VMEM)
SMEM = pl.BlockSpec(memory_space=pltpu.SMEM)


def dot(left, right):
    return jnp.dot(left, right, preferred_element_type=jnp.float32)


def spread_kernel(tokens_ref, copies_ref):
    features = tokens_ref[...].T
    for parity in range(2):
        for place in range(8):
            copies_ref[parity * 8 + place] = features[parity * 64 : parity * 64 + 64]


def spread(tokens):
    return pl.pallas_call(
        spread_kernel,
        in_specs=[VMEM],
        out_specs=VMEM,
        out_shape=jax.ShapeDtypeStruct((16, 64, 384), jnp.bfloat16),
        compiler_params=PARAMS,
        name="spread",
    )(tokens)


def contract_kernel(place_ref, features_ref, own_ref, other_ref, out_ref):
    parity = place_ref[0]
    columns = pl.ds(pl.multiple_of(place_ref[1] * BLK, BLK), BLK)
    out_ref[...] = (
        dot(features_ref[parity], own_ref[:, columns])
        + dot(features_ref[1 - parity], other_ref[:, columns])
    ).astype(out_ref.dtype)


def contract(parity, half, features, own, other, dtype):
    return pl.pallas_call(
        contract_kernel,
        in_specs=[SMEM] + [VMEM] * 3,
        out_specs=VMEM,
        out_shape=jax.ShapeDtypeStruct((BLK, BLK), dtype),
        compiler_params=PARAMS,
        name="contract",
    )(jnp.stack([parity, half]), features, own, other)


def add_kernel(keep_ref, arrived_ref, sum_ref):
    total = keep_ref[...] + arrived_ref[...].astype(jnp.float32)
    sum_ref[...] = total.astype(sum_ref.dtype)


def add(keep, arrived):
    return pl.pallas_call(
        add_kernel,
        in_specs=[VMEM] * 2,
        out_specs=VMEM,
        out_shape=jax.ShapeDtypeStruct((BLK, BLK), jnp.bfloat16),
        compiler_params=PARAMS,
        name="add",
    )(keep, arrived)


def total_kernel(shares_ref, copies_ref):
    total = shares_ref[0].astype(jnp.float32)
    for share in range(1, 16):
        total += shares_ref[share].astype(jnp.float32)
    total = total.astype(jnp.bfloat16)
    for copy in range(16):
        copies_ref[copy] = total


def total_copies(shares):
    return pl.pallas_call(
        total_kernel,
        in_specs=[VMEM],
        out_specs=VMEM,
        out_shape=jax.ShapeDtypeStruct((16, ROWS, BLK), jnp.bfloat16),
        compiler_params=PARAMS,
        name="total_copies",
    )(shares)


def roots_kernel(place_ref, block_ref, keep_ref, send_ref):
    block = block_ref[...]
    flipped = block.T
    wide = block.astype(jnp.float32)
    trace = jnp.sum(wide * wide, keepdims=True)
    row_ids = lax.broadcasted_iota(jnp.int32, (BLK, BLK), 0)
    col_ids = lax.broadcasted_iota(jnp.int32, (BLK, BLK), 1)
    diagonal = row_ids == col_ids
    damp = jnp.where(diagonal, 0.1 * trace / BLK + 1e-06, 0.0)
    base = jnp.where(diagonal, 1.25, 0.0)

    def start(gram):
        matrix = gram + damp
        inverse = lax.rsqrt(jnp.sum(matrix * matrix, keepdims=True))
        return matrix * inverse, jnp.sqrt(jnp.sqrt(inverse))

    left, left_scale = start(dot(block, flipped))
    right, right_scale = start(dot(flipped, block))
    order = lax.rem(lax.broadcasted_iota(jnp.int32, (ROWS, BLK), 0) + place_ref[1] * 16, ROWS)
    own = lax.broadcasted_iota(jnp.int32, (ROWS, BLK), 1) == order + place_ref[0]
    rows = jnp.where(own, left_scale, 0.0)
    steps = []
    for it in range(ITERS):
        factors = [(base - m * 0.25).astype(jnp.bfloat16) for m in (left, right)]
        rows = dot(rows.astype(jnp.bfloat16), factors[0])
        steps.append(factors[1])
        if it < ITERS - 1:
            squares = [dot(f, f).astype(jnp.bfloat16) for f in factors]
            fourths = [dot(s, s).astype(jnp.bfloat16) for s in squares]
            left, right = (
                dot(f, m.astype(jnp.bfloat16)) for f, m in zip(fourths, (left, right))
            )
    half = dot(rows.astype(jnp.bfloat16), block).astype(jnp.bfloat16)
    value = half * right_scale.astype(jnp.bfloat16)
    for step in steps:
        value = dot(value, step).astype(jnp.bfloat16)
    keep_ref[...] = value[:16]
    send_ref[...] = value[16:]


def apply_roots(first, core, block):
    piece = jax.ShapeDtypeStruct((16, BLK), jnp.bfloat16)
    return pl.pallas_call(
        roots_kernel,
        in_specs=[SMEM, VMEM],
        out_specs=[VMEM] * 2,
        out_shape=[piece] * 2,
        compiler_params=PARAMS,
        name="apply_roots",
    )(jnp.stack([first, core]), block)


def join_kernel(core_ref, keep_ref, arrived_ref, out_ref):
    core = core_ref[0]
    out_ref[:, pl.ds(pl.multiple_of(core * BLK, BLK), BLK)] = keep_ref[...]
    out_ref[:, pl.ds(pl.multiple_of((1 - core) * BLK, BLK), BLK)] = arrived_ref[...]


def join(core, keep, arrived):
    return pl.pallas_call(
        join_kernel,
        in_specs=[SMEM] + [VMEM] * 2,
        out_specs=VMEM,
        out_shape=jax.ShapeDtypeStruct((16, 2 * BLK), jnp.bfloat16),
        compiler_params=PARAMS,
        name="join",
    )(core[None], keep, arrived)


def swap(value, axis):
    return lax.ppermute(value, axis, [(0, 1), (1, 0)])


def exchange(value, axes):
    return lax.all_to_all(value, axes, 0, 0, tiled=True)


def body(tokens, cotangent):
    core, p, q, zp = (lax.axis_index(name) for name in ("core", "p", "q", "zp"))
    other = swap(cotangent, "p")
    features = exchange(spread(tokens), ("p", "zh", "x")).reshape(2, BLK, 384)
    sent = contract(p, 1 - core, features, cotangent, other, jnp.bfloat16)
    arrived = swap(sent, "core")
    keep = contract(p, core, features, cotangent, other, jnp.float32)
    shares = exchange(add(keep, arrived).reshape(16, ROWS, BLK), ("zr", "q", "zp"))
    block = exchange(total_copies(shares), ("p", "q", "zp")).reshape(BLK, BLK)
    first = ((q % 2) * 8 + (zp * 2 + q // 2) * 2 + p) * ROWS
    keep, sent = apply_roots(first, core, block)
    return join(core, keep, swap(sent, "core"))


def solution(mesh):
    devices = mesh.devices.reshape(2, 2, 4, 2, 2, 2, 4)
    fine = Mesh(devices, ("zr", "zp", "q", "p", "core", "zh", "x"))
    spec = P(("zr", "zp", "q", "p", "core"), ("zh", "x"))
    return jax.shard_map(
        body, mesh=fine, in_specs=(spec, spec), out_specs=spec, check_vma=False
    )
```

```python
import jax
import jax.numpy as jnp
from jax import lax
from jax.experimental import pallas as pl
from jax.experimental.pallas import tpu as pltpu
from jax.sharding import Mesh
from jax.sharding import PartitionSpec as P

BLK = 512
ITERS = 4
ROWS = 32
PARAMS = pltpu.CompilerParams(vmem_limit_bytes=48 * 1024 * 1024)
VMEM = pl.BlockSpec(memory_space=pltpu.VMEM)
SMEM = pl.BlockSpec(memory_space=pltpu.SMEM)


def dot(left, right):
    return jnp.dot(left, right, preferred_element_type=jnp.float32)


def spread_kernel(tokens_ref, copies_ref):
    features = tokens_ref[...].T
    for parity in range(2):
        for place in range(8):
            copies_ref[parity * 8 + place] = features[parity * 64 : parity * 64 + 64]


def spread(tokens):
    return pl.pallas_call(
        spread_kernel,
        in_specs=[VMEM],
        out_specs=VMEM,
        out_shape=jax.ShapeDtypeStruct((16, 64, 384), jnp.bfloat16),
        compiler_params=PARAMS,
        name="spread",
    )(tokens)


def contract_kernel(place_ref, features_ref, own_ref, other_ref, out_ref):
    parity = place_ref[0]
    columns = pl.ds(pl.multiple_of(place_ref[1] * BLK, BLK), BLK)
    features = jnp.concatenate([features_ref[parity], features_ref[1 - parity]], axis=1)
    cotangent = jnp.concatenate([own_ref[:, columns], other_ref[:, columns]], axis=0)
    out_ref[...] = dot(features, cotangent).astype(out_ref.dtype)


def contract(parity, half, features, own, other, dtype):
    return pl.pallas_call(
        contract_kernel,
        in_specs=[SMEM] + [VMEM] * 3,
        out_specs=VMEM,
        out_shape=jax.ShapeDtypeStruct((BLK, BLK), dtype),
        compiler_params=PARAMS,
        name="contract",
    )(jnp.stack([parity, half]), features, own, other)


def add_kernel(keep_ref, arrived_ref, sum_ref):
    total = keep_ref[...] + arrived_ref[...].astype(jnp.float32)
    sum_ref[...] = total.astype(sum_ref.dtype)


def add(keep, arrived):
    return pl.pallas_call(
        add_kernel,
        in_specs=[VMEM] * 2,
        out_specs=VMEM,
        out_shape=jax.ShapeDtypeStruct((BLK, BLK), jnp.bfloat16),
        compiler_params=PARAMS,
        name="add",
    )(keep, arrived)


def total_kernel(shares_ref, copies_ref):
    total = shares_ref[0].astype(jnp.float32)
    for share in range(1, 16):
        total += shares_ref[share].astype(jnp.float32)
    total = total.astype(jnp.bfloat16)
    for copy in range(16):
        copies_ref[copy] = total


def total_copies(shares):
    return pl.pallas_call(
        total_kernel,
        in_specs=[VMEM],
        out_specs=VMEM,
        out_shape=jax.ShapeDtypeStruct((16, ROWS, BLK), jnp.bfloat16),
        compiler_params=PARAMS,
        name="total_copies",
    )(shares)


def roots_kernel(place_ref, block_ref, keep_ref, send_ref):
    block = block_ref[...]
    flipped = block.T
    wide = block.astype(jnp.float32)
    trace = jnp.sum(wide * wide, keepdims=True)
    row_ids = lax.broadcasted_iota(jnp.int32, (BLK, BLK), 0)
    col_ids = lax.broadcasted_iota(jnp.int32, (BLK, BLK), 1)
    diagonal = row_ids == col_ids
    damp = jnp.where(diagonal, 0.1 * trace / BLK + 1e-06, 0.0)
    base = jnp.where(diagonal, 1.25, 0.0)

    def start(gram):
        matrix = gram + damp
        inverse = lax.rsqrt(jnp.sum(matrix * matrix, keepdims=True))
        return matrix * inverse, jnp.sqrt(jnp.sqrt(inverse))

    left, left_scale = start(dot(block, flipped))
    right, right_scale = start(dot(flipped, block))
    order = lax.rem(lax.broadcasted_iota(jnp.int32, (ROWS, BLK), 0) + place_ref[1] * 16, ROWS)
    own = lax.broadcasted_iota(jnp.int32, (ROWS, BLK), 1) == order + place_ref[0]
    rows = jnp.where(own, left_scale, 0.0)
    steps = []
    for it in range(ITERS):
        factors = [(base - m * 0.25).astype(jnp.bfloat16) for m in (left, right)]
        rows = dot(rows.astype(jnp.bfloat16), factors[0])
        steps.append(factors[1])
        if it < ITERS - 1:
            squares = [dot(f, f).astype(jnp.bfloat16) for f in factors]
            fourths = [dot(s, s).astype(jnp.bfloat16) for s in squares]
            left, right = (
                dot(f, m.astype(jnp.bfloat16)) for f, m in zip(fourths, (left, right))
            )
    half = dot(rows.astype(jnp.bfloat16), block).astype(jnp.bfloat16)
    value = half * right_scale.astype(jnp.bfloat16)
    for step in steps:
        value = dot(value, step).astype(jnp.bfloat16)
    keep_ref[...] = value[:16]
    send_ref[...] = value[16:]


def apply_roots(first, core, block):
    piece = jax.ShapeDtypeStruct((16, BLK), jnp.bfloat16)
    return pl.pallas_call(
        roots_kernel,
        in_specs=[SMEM, VMEM],
        out_specs=[VMEM] * 2,
        out_shape=[piece] * 2,
        compiler_params=PARAMS,
        name="apply_roots",
    )(jnp.stack([first, core]), block)


def join_kernel(core_ref, keep_ref, arrived_ref, out_ref):
    core = core_ref[0]
    out_ref[:, pl.ds(pl.multiple_of(core * BLK, BLK), BLK)] = keep_ref[...]
    out_ref[:, pl.ds(pl.multiple_of((1 - core) * BLK, BLK), BLK)] = arrived_ref[...]


def join(core, keep, arrived):
    return pl.pallas_call(
        join_kernel,
        in_specs=[SMEM] + [VMEM] * 2,
        out_specs=VMEM,
        out_shape=jax.ShapeDtypeStruct((16, 2 * BLK), jnp.bfloat16),
        compiler_params=PARAMS,
        name="join",
    )(core[None], keep, arrived)


def swap(value, axis):
    return lax.ppermute(value, axis, [(0, 1), (1, 0)])


def exchange(value, axes):
    return lax.all_to_all(value, axes, 0, 0, tiled=True)


def partner(y, core):
    return (y + 1 if (y + core) % 2 == 0 else y - 1) % 8


def pair_groups():
    groups = []
    for core in range(2):
        for even in range(0, 8, 2):
            pair = (even, partner(even, core))
            groups.append(
                [(y * 2 + core) * 8 + feature for y in pair for feature in range(8)]
            )
    return groups


def body(tokens, cotangent):
    core, p, q, zp = (lax.axis_index(name) for name in ("core", "p", "q", "zp"))
    pairs = [(y * 2 + k, partner(y, k) * 2 + k) for y in range(8) for k in range(2)]
    other = lax.ppermute(cotangent, ("q", "p", "core"), pairs)
    features = lax.all_to_all(
        spread(tokens),
        ("q", "p", "core", "zh", "x"),
        0,
        0,
        axis_index_groups=pair_groups(),
        tiled=True,
    ).reshape(2, BLK, 384)
    sent = contract(p, 1 - core, features, cotangent, other, jnp.bfloat16)
    arrived = swap(sent, "core")
    keep = contract(p, core, features, cotangent, other, jnp.float32)
    shares = exchange(add(keep, arrived).reshape(16, ROWS, BLK), ("zr", "q", "zp"))
    block = exchange(total_copies(shares), ("p", "q", "zp")).reshape(BLK, BLK)
    first = ((q % 2) * 8 + (zp * 2 + q // 2) * 2 + p) * ROWS
    keep, sent = apply_roots(first, core, block)
    return join(core, keep, swap(sent, "core"))


def solution(mesh):
    devices = mesh.devices.reshape(2, 2, 4, 2, 2, 2, 4)
    fine = Mesh(devices, ("zr", "zp", "q", "p", "core", "zh", "x"))
    spec = P(("zr", "zp", "q", "p", "core"), ("zh", "x"))
    return jax.shard_map(
        body, mesh=fine, in_specs=(spec, spec), out_specs=spec, check_vma=False
    )
```

```python
import jax
import jax.numpy as jnp
from jax import lax
from jax.experimental import pallas as pl
from jax.experimental.pallas import tpu as pltpu
from jax.sharding import Mesh
from jax.sharding import PartitionSpec as P

BLK = 512
ITERS = 4
ROWS = 32
PARAMS = pltpu.CompilerParams(vmem_limit_bytes=24 * 1024 * 1024)
VMEM = pl.BlockSpec(memory_space=pltpu.VMEM)
SMEM = pl.BlockSpec(memory_space=pltpu.SMEM)
EARLY = pl.CostEstimate(flops=10**10, bytes_accessed=3 << 20, transcendentals=0)


def dot(left, right):
    return jnp.dot(left, right, preferred_element_type=jnp.float32)


def spread_kernel(tokens_ref, copies_ref):
    features = tokens_ref[...].T
    for parity in range(2):
        for place in range(8):
            copies_ref[parity * 8 + place] = features[parity * 64 : parity * 64 + 64]


def spread(tokens):
    return pl.pallas_call(
        spread_kernel,
        in_specs=[VMEM],
        out_specs=VMEM,
        out_shape=jax.ShapeDtypeStruct((16, 64, 384), jnp.bfloat16),
        compiler_params=PARAMS,
        name="spread",
    )(tokens)


def stack_kernel(parity_ref, own_ref, other_ref, out_ref, sems):
    parity = parity_ref[0]
    copies = [
        pltpu.make_async_copy(
            source, out_ref.at[pl.ds(pl.multiple_of(place * 384, 384), 384)], sems.at[i]
        )
        for i, (source, place) in enumerate(((own_ref, parity), (other_ref, 1 - parity)))
    ]
    for copy in copies:
        copy.start()
    for copy in copies:
        copy.wait()


def stack(parity, own, other):
    return pl.pallas_call(
        stack_kernel,
        in_specs=[SMEM] + [pl.BlockSpec(memory_space=pl.ANY)] * 2,
        out_specs=VMEM,
        out_shape=jax.ShapeDtypeStruct((768, 2 * BLK), jnp.bfloat16),
        scratch_shapes=[pltpu.SemaphoreType.DMA((2,))],
        compiler_params=PARAMS,
        cost_estimate=EARLY,
        name="stack",
    )(parity[None], own, other)


def contract_kernel(half_ref, features_ref, cotangent_ref, out_ref):
    rows = pl.ds(pl.multiple_of(half_ref[0] * ROWS, ROWS), ROWS)
    features = jnp.concatenate(
        [features_ref[parity, :, rows, :].reshape(256, 384) for parity in range(2)], axis=1
    )
    out_ref[...] = dot(features, cotangent_ref[...]).astype(out_ref.dtype)


def contract(half, features, cotangent, dtype):
    return pl.pallas_call(
        contract_kernel,
        in_specs=[SMEM] + [VMEM] * 2,
        out_specs=VMEM,
        out_shape=jax.ShapeDtypeStruct((256, 2 * BLK), dtype),
        compiler_params=PARAMS,
        name="contract",
    )(half[None], features, cotangent)


def add_kernel(keep_ref, arrived_ref, shares_ref):
    for place in range(8):
        rows = slice(place * ROWS, place * ROWS + ROWS)
        total = (keep_ref[rows] + arrived_ref[rows].astype(jnp.float32)).astype(jnp.bfloat16)
        shares_ref[place * 2] = total[:, :BLK]
        shares_ref[place * 2 + 1] = total[:, BLK:]


def add(keep, arrived):
    return pl.pallas_call(
        add_kernel,
        in_specs=[VMEM] * 2,
        out_specs=VMEM,
        out_shape=jax.ShapeDtypeStruct((16, ROWS, BLK), jnp.bfloat16),
        compiler_params=PARAMS,
        name="add",
    )(keep, arrived)


def total_kernel(shares_ref, copies_ref):
    total = shares_ref[0].astype(jnp.float32)
    for share in range(1, 16):
        total += shares_ref[share].astype(jnp.float32)
    total = total.astype(jnp.bfloat16)
    for copy in range(8):
        copies_ref[copy] = total


def total_copies(shares):
    return pl.pallas_call(
        total_kernel,
        in_specs=[VMEM],
        out_specs=VMEM,
        out_shape=jax.ShapeDtypeStruct((8, ROWS, BLK), jnp.bfloat16),
        compiler_params=PARAMS,
        name="total_copies",
    )(shares)


def roots_kernel(place_ref, own_ref, arrived_ref, keep_ref, send_ref):
    block = jnp.concatenate([own_ref[...], arrived_ref[...]], axis=0)
    flipped = block.T
    wide = block.astype(jnp.float32)
    trace = jnp.sum(wide * wide, keepdims=True)
    row_ids = lax.broadcasted_iota(jnp.int32, (BLK, BLK), 0)
    col_ids = lax.broadcasted_iota(jnp.int32, (BLK, BLK), 1)
    diagonal = row_ids == col_ids
    damp = jnp.where(diagonal, 0.1 * trace / BLK + 1e-06, 0.0)
    base = jnp.where(diagonal, 1.25, 0.0)

    def start(gram):
        matrix = gram + damp
        inverse = lax.rsqrt(jnp.sum(matrix * matrix, keepdims=True))
        return matrix * inverse, jnp.sqrt(jnp.sqrt(inverse))

    left, left_scale = start(dot(block, flipped))
    right, right_scale = start(dot(flipped, block))
    ids = lax.broadcasted_iota(jnp.int32, (ROWS, BLK), 0)
    picked = jnp.where(ids < 16, ids + place_ref[0], ids - 16 + place_ref[1])
    rows = jnp.where(
        lax.broadcasted_iota(jnp.int32, (ROWS, BLK), 1) == picked, left_scale, 0.0
    )
    steps = []
    for it in range(ITERS):
        factors = [(base - m * 0.25).astype(jnp.bfloat16) for m in (left, right)]
        rows = dot(rows.astype(jnp.bfloat16), factors[0])
        steps.append(factors[1])
        if it < ITERS - 1:
            squares = [dot(f, f).astype(jnp.bfloat16) for f in factors]
            fourths = [dot(s, s).astype(jnp.bfloat16) for s in squares]
            left, right = (
                dot(f, m.astype(jnp.bfloat16)) for f, m in zip(fourths, (left, right))
            )
    half = dot(rows.astype(jnp.bfloat16), block).astype(jnp.bfloat16)
    value = half * right_scale.astype(jnp.bfloat16)
    for step in steps:
        value = dot(value, step).astype(jnp.bfloat16)
    keep_ref[...] = value[:16]
    send_ref[...] = value[16:]


def apply_roots(places, own, arrived):
    piece = jax.ShapeDtypeStruct((16, BLK), jnp.bfloat16)
    return pl.pallas_call(
        roots_kernel,
        in_specs=[SMEM] + [VMEM] * 2,
        out_specs=[VMEM] * 2,
        out_shape=[piece] * 2,
        compiler_params=PARAMS,
        name="apply_roots",
    )(places, own, arrived)


def join_kernel(column_ref, keep_ref, arrived_ref, out_ref):
    column = column_ref[0]
    out_ref[:, pl.ds(pl.multiple_of(column * BLK, BLK), BLK)] = keep_ref[...]
    out_ref[:, pl.ds(pl.multiple_of((1 - column) * BLK, BLK), BLK)] = arrived_ref[...]


def join(column, keep, arrived):
    return pl.pallas_call(
        join_kernel,
        in_specs=[SMEM] + [VMEM] * 2,
        out_specs=VMEM,
        out_shape=jax.ShapeDtypeStruct((16, 2 * BLK), jnp.bfloat16),
        compiler_params=PARAMS,
        name="join",
    )(column[None], keep, arrived)


def swap(value, axis):
    return lax.ppermute(value, axis, [(0, 1), (1, 0)])


def exchange(value, axes):
    return lax.all_to_all(value, axes, 0, 0, tiled=True)


def partner(y, core):
    return (y + 1 if (y + core) % 2 == 0 else y - 1) % 8


def pair_groups():
    groups = []
    for core in range(2):
        for even in range(0, 8, 2):
            pair = (even, partner(even, core))
            groups.append(
                [(y * 2 + core) * 8 + feature for y in pair for feature in range(8)]
            )
    return groups


def body(tokens, cotangent):
    core, p, q, zp = (lax.axis_index(name) for name in ("core", "p", "q", "zp"))
    pairs = [(y * 2 + k, partner(y, k) * 2 + k) for y in range(8) for k in range(2)]
    other = lax.ppermute(cotangent, ("q", "p", "core"), pairs)
    features = lax.all_to_all(
        spread(tokens),
        ("q", "p", "core", "zh", "x"),
        0,
        0,
        axis_index_groups=pair_groups(),
        tiled=True,
    ).reshape(2, 8, 64, 384)
    both = stack(p, cotangent, other)
    arrived = swap(contract(1 - core, features, both, jnp.bfloat16), "core")
    keep = contract(core, features, both, jnp.float32)
    shares = exchange(add(keep, arrived), ("zr", "q", "zp"))
    own = exchange(total_copies(shares), ("p", "q")).reshape(256, BLK)
    place = jnp.where(p == core, 0, 256) + ((q % 2) * 4 + q // 2) * ROWS + core * 16
    places = jnp.stack([place + zp * 64, place + (1 - zp) * 64])
    keep, sent = apply_roots(places, own, swap(own, "core"))
    return join(zp, keep, swap(sent, "zp"))


def solution(mesh):
    devices = mesh.devices.reshape(2, 2, 4, 2, 2, 2, 4)
    fine = Mesh(devices, ("zr", "zp", "q", "p", "core", "zh", "x"))
    spec = P(("zr", "zp", "q", "p", "core"), ("zh", "x"))
    return jax.shard_map(
        body, mesh=fine, in_specs=(spec, spec), out_specs=spec, check_vma=False
    )
```

```python
import jax
import jax.numpy as jnp
from jax import lax
from jax.experimental import pallas as pl
from jax.experimental.pallas import tpu as pltpu
from jax.sharding import Mesh
from jax.sharding import PartitionSpec as P

BLK = 512
HALF = 256
ITERS = 4
ROWS = 32
PARAMS = pltpu.CompilerParams(vmem_limit_bytes=24 * 1024 * 1024)
VMEM = pl.BlockSpec(memory_space=pltpu.VMEM)
SMEM = pl.BlockSpec(memory_space=pltpu.SMEM)


def dot(left, right):
    return jnp.dot(left, right, preferred_element_type=jnp.float32)


def spread_kernel(tokens_ref, copies_ref):
    features = tokens_ref[...].T
    for parity in range(2):
        for place in range(8):
            copies_ref[parity * 8 + place] = features[parity * 64 : parity * 64 + 64]


def spread(tokens):
    return pl.pallas_call(
        spread_kernel,
        in_specs=[VMEM],
        out_specs=VMEM,
        out_shape=jax.ShapeDtypeStruct((16, 64, 384), jnp.bfloat16),
        compiler_params=PARAMS,
        name="spread",
    )(tokens)


def stack_kernel(parity_ref, own_ref, other_ref, out_ref, sems):
    parity = parity_ref[0]
    copies = [
        pltpu.make_async_copy(
            source, out_ref.at[pl.ds(pl.multiple_of(place * 384, 384), 384)], sems.at[i]
        )
        for i, (source, place) in enumerate(((own_ref, parity), (other_ref, 1 - parity)))
    ]
    for copy in copies:
        copy.start()
    for copy in copies:
        copy.wait()


def stack(parity, own, other):
    return pl.pallas_call(
        stack_kernel,
        in_specs=[SMEM] + [pl.BlockSpec(memory_space=pl.ANY)] * 2,
        out_specs=VMEM,
        out_shape=jax.ShapeDtypeStruct((768, 2 * BLK), jnp.bfloat16),
        scratch_shapes=[pltpu.SemaphoreType.DMA((2,))],
        compiler_params=PARAMS,
        name="stack",
    )(parity[None], own, other)


def contract_kernel(half_ref, features_ref, cotangent_ref, out_ref):
    rows = pl.ds(pl.multiple_of(half_ref[0] * ROWS, ROWS), ROWS)
    features = jnp.concatenate(
        [features_ref[parity, :, rows, :].reshape(256, 384) for parity in range(2)], axis=1
    )
    out_ref[...] = dot(features, cotangent_ref[...]).astype(out_ref.dtype)


def contract(half, features, cotangent, dtype):
    return pl.pallas_call(
        contract_kernel,
        in_specs=[SMEM] + [VMEM] * 2,
        out_specs=VMEM,
        out_shape=jax.ShapeDtypeStruct((256, 2 * BLK), dtype),
        compiler_params=PARAMS,
        name="contract",
    )(half[None], features, cotangent)


def add_kernel(keep_ref, arrived_ref, shares_ref):
    for place in range(8):
        rows = slice(place * ROWS, place * ROWS + ROWS)
        total = (keep_ref[rows] + arrived_ref[rows].astype(jnp.float32)).astype(jnp.bfloat16)
        shares_ref[place * 2] = total[:, :BLK]
        shares_ref[place * 2 + 1] = total[:, BLK:]


def add(keep, arrived):
    return pl.pallas_call(
        add_kernel,
        in_specs=[VMEM] * 2,
        out_specs=VMEM,
        out_shape=jax.ShapeDtypeStruct((16, ROWS, BLK), jnp.bfloat16),
        compiler_params=PARAMS,
        name="add",
    )(keep, arrived)


def total_kernel(shares_ref, copies_ref):
    total = shares_ref[0].astype(jnp.float32)
    for share in range(1, 16):
        total += shares_ref[share].astype(jnp.float32)
    total = total.astype(jnp.bfloat16)
    for copy in range(8):
        copies_ref[copy] = total


def total_copies(shares):
    return pl.pallas_call(
        total_kernel,
        in_specs=[VMEM],
        out_specs=VMEM,
        out_shape=jax.ShapeDtypeStruct((8, ROWS, BLK), jnp.bfloat16),
        compiler_params=PARAMS,
        name="total_copies",
    )(shares)


def symmetric_product(left, right, store, rows=None):
    top = left[:HALF, :] if rows is None else jnp.concatenate([left[:HALF, :], rows], axis=0)
    top = dot(top, right[...])
    store(0, 0, top[:HALF, :HALF])
    store(0, HALF, top[:HALF, HALF:])
    store(HALF, HALF, dot(left[HALF:, :], right[:, HALF:]))
    return top[HALF:].astype(jnp.bfloat16)


def put(ref, i, j, value):
    ref[i : i + HALF, j : j + HALF] = value
    if i != j:
        ref[j : j + HALF, i : i + HALF] = value.T


def rounded(ref):
    return lambda i, j, value: put(ref, i, j, value.astype(jnp.bfloat16))


def roots_kernel(
    place_ref, own_ref, arrived_ref, keep_ref, send_ref, block_ref, flipped_ref, *scratch
):
    lgram, rgram, lstep, rstep, lsquare, rsquare, lfourth, rfourth, lmat, rmat, rroot = scratch
    block_ref[:HALF, :] = own_ref[...]
    block_ref[HALF:, :] = arrived_ref[...]
    flipped_ref[...] = block_ref[...].T
    wide = block_ref[...].astype(jnp.float32)
    trace = jnp.sum(wide * wide, keepdims=True)
    damp = 0.1 * trace / BLK + 1e-06
    diagonal = lax.broadcasted_iota(jnp.int32, (HALF, HALF), 0) == lax.broadcasted_iota(
        jnp.int32, (HALF, HALF), 1
    )
    base = jnp.where(diagonal, 1.25, 0.0)

    def set_step(step, i, j, value):
        put(step, i, j, ((base if i == j else 0.0) - value * 0.25).astype(jnp.bfloat16))

    def start(left, right, gram, mat, step):
        parts = []

        def store(i, j, value):
            gram[i : i + HALF, j : j + HALF] = value
            if i == j:
                value = value + jnp.where(diagonal, damp, 0.0)
            parts.append(jnp.sum(value * value, keepdims=True) * (1.0 if i == j else 2.0))

        symmetric_product(left, right, store)
        inverse = lax.rsqrt(parts[0] + parts[1] + parts[2])
        for i, j in ((0, 0), (0, HALF), (HALF, HALF)):
            value = gram[i : i + HALF, j : j + HALF]
            if i == j:
                value = value + jnp.where(diagonal, damp, 0.0)
            value = value * inverse
            put(mat, i, j, value.astype(jnp.bfloat16))
            set_step(step, i, j, value)
        return jnp.sqrt(jnp.sqrt(inverse))

    lscale = start(block_ref, flipped_ref, lgram, lmat, lstep)
    rscale = start(flipped_ref, block_ref, rgram, rmat, rstep)
    ids = lax.broadcasted_iota(jnp.int32, (ROWS, BLK), 0)
    picked = jnp.where(ids < 16, ids + place_ref[0], ids - 16 + place_ref[1])
    columns = lax.broadcasted_iota(jnp.int32, (ROWS, BLK), 1)
    rows = jnp.where(columns == picked, lscale, 0.0).astype(jnp.bfloat16)
    rroot[...] = rstep[...] * rscale.astype(jnp.bfloat16)
    for it in range(ITERS - 1):
        rows = symmetric_product(lstep, lstep, rounded(lsquare), rows)
        symmetric_product(rstep, rstep, rounded(rsquare))
        if it > 0:
            rroot[...] = dot(rroot[...], rstep[...]).astype(jnp.bfloat16)
        symmetric_product(lsquare, lsquare, rounded(lfourth))
        symmetric_product(rsquare, rsquare, rounded(rfourth))
        for fourth, mat, step in ((lfourth, lmat, lstep), (rfourth, rmat, rstep)):
            parts = []
            symmetric_product(fourth, mat, lambda i, j, value: parts.append((i, j, value)))
            for i, j, value in parts:
                if it < ITERS - 2:
                    put(mat, i, j, value.astype(jnp.bfloat16))
                set_step(step, i, j, value)
    rows = dot(rows, lstep[...]).astype(jnp.bfloat16)
    half = dot(rows, block_ref[...]).astype(jnp.bfloat16)
    rroot[...] = dot(rroot[...], rstep[...]).astype(jnp.bfloat16)
    value = dot(half, rroot[...]).astype(jnp.bfloat16)
    keep_ref[...] = value[:16]
    send_ref[...] = value[16:]


def apply_roots(places, own, arrived):
    piece = jax.ShapeDtypeStruct((16, BLK), jnp.bfloat16)
    narrow = pltpu.VMEM((BLK, BLK), jnp.bfloat16)
    return pl.pallas_call(
        roots_kernel,
        in_specs=[SMEM] + [VMEM] * 2,
        out_specs=[VMEM] * 2,
        out_shape=[piece] * 2,
        scratch_shapes=[narrow] * 2 + [pltpu.VMEM((BLK, BLK), jnp.float32)] * 2 + [narrow] * 9,
        compiler_params=PARAMS,
        name="apply_roots",
    )(places, own, arrived)


def join_kernel(column_ref, keep_ref, arrived_ref, out_ref):
    column = column_ref[0]
    out_ref[:, pl.ds(pl.multiple_of(column * BLK, BLK), BLK)] = keep_ref[...]
    out_ref[:, pl.ds(pl.multiple_of((1 - column) * BLK, BLK), BLK)] = arrived_ref[...]


def join(column, keep, arrived):
    return pl.pallas_call(
        join_kernel,
        in_specs=[SMEM] + [VMEM] * 2,
        out_specs=VMEM,
        out_shape=jax.ShapeDtypeStruct((16, 2 * BLK), jnp.bfloat16),
        compiler_params=PARAMS,
        name="join",
    )(column[None], keep, arrived)


def swap(value, axis):
    return lax.ppermute(value, axis, [(0, 1), (1, 0)])


def exchange(value, axes):
    return lax.all_to_all(value, axes, 0, 0, tiled=True)


def partner(y, core):
    return (y + 1 if (y + core) % 2 == 0 else y - 1) % 8


def pair_groups():
    groups = []
    for core in range(2):
        for even in range(0, 8, 2):
            pair = (even, partner(even, core))
            groups.append(
                [(y * 2 + core) * 8 + feature for y in pair for feature in range(8)]
            )
    return groups


def body(tokens, cotangent):
    core, p, q, zp = (lax.axis_index(name) for name in ("core", "p", "q", "zp"))
    pairs = [(y * 2 + k, partner(y, k) * 2 + k) for y in range(8) for k in range(2)]
    other = lax.ppermute(cotangent, ("q", "p", "core"), pairs)
    features = lax.all_to_all(
        spread(tokens),
        ("q", "p", "core", "zh", "x"),
        0,
        0,
        axis_index_groups=pair_groups(),
        tiled=True,
    ).reshape(2, 8, 64, 384)
    both = stack(p, cotangent, other)
    arrived = swap(contract(1 - core, features, both, jnp.bfloat16), "core")
    keep = contract(core, features, both, jnp.float32)
    shares = exchange(add(keep, arrived), ("zr", "q", "zp"))
    own = exchange(total_copies(shares), ("p", "q")).reshape(256, BLK)
    place = jnp.where(p == core, 0, 256) + ((q % 2) * 4 + q // 2) * ROWS + core * 16
    places = jnp.stack([place + zp * 64, place + (1 - zp) * 64])
    keep, sent = apply_roots(places, own, swap(own, "core"))
    return join(zp, keep, swap(sent, "zp"))


def solution(mesh):
    devices = mesh.devices.reshape(2, 2, 4, 2, 2, 2, 4)
    fine = Mesh(devices, ("zr", "zp", "q", "p", "core", "zh", "x"))
    spec = P(("zr", "zp", "q", "p", "core"), ("zh", "x"))
    return jax.shard_map(
        body, mesh=fine, in_specs=(spec, spec), out_specs=spec, check_vma=False
    )
```

```python
import jax
import jax.numpy as jnp
from jax import lax
from jax.experimental import pallas as pl
from jax.experimental.pallas import tpu as pltpu
from jax.sharding import Mesh
from jax.sharding import PartitionSpec as P

BLK = 512
HALF = 256
ITERS = 4
ROWS = 32
PARAMS = pltpu.CompilerParams(vmem_limit_bytes=24 * 1024 * 1024)
VMEM = pl.BlockSpec(memory_space=pltpu.VMEM)
SMEM = pl.BlockSpec(memory_space=pltpu.SMEM)
EARLY = pl.CostEstimate(flops=7 * 10**9, bytes_accessed=3 << 20, transcendentals=0)


def dot(left, right):
    return jnp.dot(left, right, preferred_element_type=jnp.float32)


def turn_kernel(tokens_ref, turned_ref):
    turned_ref[...] = tokens_ref[...].T


def turn(tokens):
    return pl.pallas_call(
        turn_kernel,
        in_specs=[VMEM],
        out_specs=VMEM,
        out_shape=jax.ShapeDtypeStruct((128, 384), jnp.bfloat16),
        compiler_params=PARAMS,
        name="turn",
    )(tokens)


def spread_kernel(zh_ref, turned_ref, far_ref, copies_ref):
    zh = zh_ref[0]
    for features, at in ((turned_ref[...], zh), (far_ref[...].T, 1 - zh)):
        for parity in range(2):
            for place in range(4):
                copies_ref[parity * 4 + place, at] = features[parity * 64 : parity * 64 + 64]


def spread(zh, turned, far):
    return pl.pallas_call(
        spread_kernel,
        in_specs=[SMEM] + [VMEM] * 2,
        out_specs=VMEM,
        out_shape=jax.ShapeDtypeStruct((8, 2, 64, 384), jnp.bfloat16),
        compiler_params=PARAMS,
        name="spread",
    )(zh[None], turned, far)


def stack_kernel(parity_ref, own_ref, other_ref, out_ref, sems):
    parity = parity_ref[0]
    copies = [
        pltpu.make_async_copy(
            source, out_ref.at[pl.ds(pl.multiple_of(place * 384, 384), 384)], sems.at[i]
        )
        for i, (source, place) in enumerate(((own_ref, parity), (other_ref, 1 - parity)))
    ]
    for copy in copies:
        copy.start()
    for copy in copies:
        copy.wait()


def stack(parity, own, other):
    return pl.pallas_call(
        stack_kernel,
        in_specs=[SMEM] + [pl.BlockSpec(memory_space=pl.ANY)] * 2,
        out_specs=VMEM,
        out_shape=jax.ShapeDtypeStruct((768, 2 * BLK), jnp.bfloat16),
        scratch_shapes=[pltpu.SemaphoreType.DMA((2,))],
        compiler_params=PARAMS,
        cost_estimate=EARLY,
        name="stack",
    )(parity[None], own, other)


def contract_kernel(half_ref, features_ref, cotangent_ref, out_ref):
    rows = pl.ds(pl.multiple_of(half_ref[0] * ROWS, ROWS), ROWS)
    features = jnp.concatenate(
        [
            jnp.concatenate(
                [features_ref[parity, :, zh, rows, :].reshape(128, 384) for zh in range(2)], axis=0
            )
            for parity in range(2)
        ],
        axis=1,
    )
    out_ref[...] = dot(features, cotangent_ref[...]).astype(out_ref.dtype)


def contract(half, features, cotangent, dtype):
    return pl.pallas_call(
        contract_kernel,
        in_specs=[SMEM] + [VMEM] * 2,
        out_specs=VMEM,
        out_shape=jax.ShapeDtypeStruct((256, 2 * BLK), dtype),
        compiler_params=PARAMS,
        name="contract",
    )(half[None], features, cotangent)


def add_kernel(keep_ref, arrived_ref, shares_ref):
    for place in range(8):
        rows = slice(place * ROWS, place * ROWS + ROWS)
        total = (keep_ref[rows] + arrived_ref[rows].astype(jnp.float32)).astype(jnp.bfloat16)
        shares_ref[place * 2] = total[:, :BLK]
        shares_ref[place * 2 + 1] = total[:, BLK:]


def add(keep, arrived):
    return pl.pallas_call(
        add_kernel,
        in_specs=[VMEM] * 2,
        out_specs=VMEM,
        out_shape=jax.ShapeDtypeStruct((16, ROWS, BLK), jnp.bfloat16),
        compiler_params=PARAMS,
        name="add",
    )(keep, arrived)


def total_kernel(shares_ref, copies_ref):
    total = shares_ref[0].astype(jnp.float32)
    for share in range(1, 16):
        total += shares_ref[share].astype(jnp.float32)
    total = total.astype(jnp.bfloat16)
    for copy in range(8):
        copies_ref[copy] = total


def total_copies(shares):
    return pl.pallas_call(
        total_kernel,
        in_specs=[VMEM],
        out_specs=VMEM,
        out_shape=jax.ShapeDtypeStruct((8, ROWS, BLK), jnp.bfloat16),
        compiler_params=PARAMS,
        name="total_copies",
    )(shares)


def symmetric_product(left, right, store, rows=None):
    top = left[:HALF, :] if rows is None else jnp.concatenate([left[:HALF, :], rows], axis=0)
    top = dot(top, right[...])
    store(0, 0, top[:HALF, :HALF])
    store(0, HALF, top[:HALF, HALF:])
    store(HALF, HALF, dot(left[HALF:, :], right[:, HALF:]))
    return top[HALF:].astype(jnp.bfloat16)


def put(ref, i, j, value):
    ref[i : i + HALF, j : j + HALF] = value
    if i != j:
        ref[j : j + HALF, i : i + HALF] = value.T


def rounded(ref):
    return lambda i, j, value: put(ref, i, j, value.astype(jnp.bfloat16))


def roots_kernel(
    place_ref, own_ref, arrived_ref, keep_ref, send_ref, block_ref, flipped_ref, *scratch
):
    lgram, rgram, lstep, rstep, lsquare, rsquare, lfourth, rfourth, lmat, rmat, rroot = scratch
    block_ref[:HALF, :] = own_ref[...]
    block_ref[HALF:, :] = arrived_ref[...]
    flipped_ref[...] = block_ref[...].T
    wide = block_ref[...].astype(jnp.float32)
    trace = jnp.sum(wide * wide, keepdims=True)
    damp = 0.1 * trace / BLK + 1e-06
    diagonal = lax.broadcasted_iota(jnp.int32, (HALF, HALF), 0) == lax.broadcasted_iota(
        jnp.int32, (HALF, HALF), 1
    )
    base = jnp.where(diagonal, 1.25, 0.0)

    def set_step(step, i, j, value):
        put(step, i, j, ((base if i == j else 0.0) - value * 0.25).astype(jnp.bfloat16))

    def start(left, right, gram, mat, step):
        parts = []

        def store(i, j, value):
            gram[i : i + HALF, j : j + HALF] = value
            if i == j:
                value = value + jnp.where(diagonal, damp, 0.0)
            parts.append(jnp.sum(value * value, keepdims=True) * (1.0 if i == j else 2.0))

        symmetric_product(left, right, store)
        inverse = lax.rsqrt(parts[0] + parts[1] + parts[2])
        for i, j in ((0, 0), (0, HALF), (HALF, HALF)):
            value = gram[i : i + HALF, j : j + HALF]
            if i == j:
                value = value + jnp.where(diagonal, damp, 0.0)
            value = value * inverse
            put(mat, i, j, value.astype(jnp.bfloat16))
            set_step(step, i, j, value)
        return jnp.sqrt(jnp.sqrt(inverse))

    lscale = start(block_ref, flipped_ref, lgram, lmat, lstep)
    rscale = start(flipped_ref, block_ref, rgram, rmat, rstep)
    ids = lax.broadcasted_iota(jnp.int32, (ROWS, BLK), 0)
    picked = jnp.where(ids < 16, ids + place_ref[0], ids - 16 + place_ref[1])
    columns = lax.broadcasted_iota(jnp.int32, (ROWS, BLK), 1)
    rows = jnp.where(columns == picked, lscale, 0.0).astype(jnp.bfloat16)
    rroot[...] = rstep[...] * rscale.astype(jnp.bfloat16)
    for it in range(ITERS - 1):
        rows = symmetric_product(lstep, lstep, rounded(lsquare), rows)
        symmetric_product(rstep, rstep, rounded(rsquare))
        if it > 0:
            rroot[...] = dot(rroot[...], rstep[...]).astype(jnp.bfloat16)
        symmetric_product(lsquare, lsquare, rounded(lfourth))
        symmetric_product(rsquare, rsquare, rounded(rfourth))
        for fourth, mat, step in ((lfourth, lmat, lstep), (rfourth, rmat, rstep)):
            parts = []
            symmetric_product(fourth, mat, lambda i, j, value: parts.append((i, j, value)))
            for i, j, value in parts:
                if it < ITERS - 2:
                    put(mat, i, j, value.astype(jnp.bfloat16))
                set_step(step, i, j, value)
    rows = dot(rows, lstep[...]).astype(jnp.bfloat16)
    half = dot(rows, block_ref[...]).astype(jnp.bfloat16)
    rroot[...] = dot(rroot[...], rstep[...]).astype(jnp.bfloat16)
    value = dot(half, rroot[...]).astype(jnp.bfloat16)
    keep_ref[...] = value[:16]
    send_ref[...] = value[16:]


def apply_roots(places, own, arrived):
    piece = jax.ShapeDtypeStruct((16, BLK), jnp.bfloat16)
    narrow = pltpu.VMEM((BLK, BLK), jnp.bfloat16)
    return pl.pallas_call(
        roots_kernel,
        in_specs=[SMEM] + [VMEM] * 2,
        out_specs=[VMEM] * 2,
        out_shape=[piece] * 2,
        scratch_shapes=[narrow] * 2 + [pltpu.VMEM((BLK, BLK), jnp.float32)] * 2 + [narrow] * 9,
        compiler_params=PARAMS,
        name="apply_roots",
    )(places, own, arrived)


def join_kernel(column_ref, keep_ref, arrived_ref, out_ref):
    column = column_ref[0]
    out_ref[:, pl.ds(pl.multiple_of(column * BLK, BLK), BLK)] = keep_ref[...]
    out_ref[:, pl.ds(pl.multiple_of((1 - column) * BLK, BLK), BLK)] = arrived_ref[...]


def join(column, keep, arrived):
    return pl.pallas_call(
        join_kernel,
        in_specs=[SMEM] + [VMEM] * 2,
        out_specs=VMEM,
        out_shape=jax.ShapeDtypeStruct((16, 2 * BLK), jnp.bfloat16),
        compiler_params=PARAMS,
        name="join",
    )(column[None], keep, arrived)


def swap(value, axis):
    return lax.ppermute(value, axis, [(0, 1), (1, 0)])


def exchange(value, axes):
    return lax.all_to_all(value, axes, 0, 0, tiled=True)


def partner(y, core):
    return (y + 1 if (y + core) % 2 == 0 else y - 1) % 8


def pair_groups():
    groups = []
    for core in range(2):
        for even in range(0, 8, 2):
            pair = (even, partner(even, core))
            for zh in range(2):
                groups.append(
                    [(y * 2 + core) * 8 + zh * 4 + x for y in pair for x in range(4)]
                )
    return groups


def body(tokens, cotangent):
    core, p, q, zp = (lax.axis_index(name) for name in ("core", "p", "q", "zp"))
    pairs = [(y * 2 + k, partner(y, k) * 2 + k) for y in range(8) for k in range(2)]
    other = lax.ppermute(cotangent, ("q", "p", "core"), pairs)
    features = lax.all_to_all(
        spread(lax.axis_index("zh"), turn(tokens), swap(tokens, "zh")),
        ("q", "p", "core", "zh", "x"),
        0,
        0,
        axis_index_groups=pair_groups(),
        tiled=True,
    ).reshape(2, 4, 2, 64, 384)
    both = stack(p, cotangent, other)
    arrived = swap(contract(1 - core, features, both, jnp.bfloat16), "core")
    keep = contract(core, features, both, jnp.float32)
    shares = exchange(add(keep, arrived), ("zr", "q", "zp"))
    own = exchange(total_copies(shares), ("p", "q")).reshape(256, BLK)
    place = jnp.where(p == core, 0, 256) + ((q % 2) * 4 + q // 2) * ROWS + core * 16
    places = jnp.stack([place + zp * 64, place + (1 - zp) * 64])
    keep, sent = apply_roots(places, own, swap(own, "core"))
    return join(zp, keep, swap(sent, "zp"))


def solution(mesh):
    devices = mesh.devices.reshape(2, 2, 4, 2, 2, 2, 4)
    fine = Mesh(devices, ("zr", "zp", "q", "p", "core", "zh", "x"))
    spec = P(("zr", "zp", "q", "p", "core"), ("zh", "x"))
    return jax.shard_map(
        body, mesh=fine, in_specs=(spec, spec), out_specs=spec, check_vma=False
    )
```

```python
import jax
import jax.numpy as jnp
from jax import lax
from jax.experimental import pallas as pl
from jax.experimental.pallas import tpu as pltpu
from jax.sharding import Mesh
from jax.sharding import PartitionSpec as P

BLK = 512
HALF = 256
ITERS = 4
ROWS = 32
PARAMS = pltpu.CompilerParams(vmem_limit_bytes=24 * 1024 * 1024)
VMEM = pl.BlockSpec(memory_space=pltpu.VMEM)
SMEM = pl.BlockSpec(memory_space=pltpu.SMEM)
EARLY = pl.CostEstimate(flops=7 * 10**9, bytes_accessed=3 << 20, transcendentals=0)


def dot(left, right):
    return jnp.dot(left, right, preferred_element_type=jnp.float32)


def turn_kernel(tokens_ref, turned_ref):
    turned_ref[...] = tokens_ref[...].T


def turn(tokens):
    return pl.pallas_call(
        turn_kernel,
        in_specs=[VMEM],
        out_specs=VMEM,
        out_shape=jax.ShapeDtypeStruct((128, 384), jnp.bfloat16),
        compiler_params=PARAMS,
        name="turn",
    )(tokens)


def spread_kernel(zh_ref, turned_ref, far_ref, copies_ref):
    zh = zh_ref[0]
    for features, at in ((turned_ref[...], zh), (far_ref[...].T, 1 - zh)):
        for parity in range(2):
            for place in range(4):
                copies_ref[parity * 4 + place, at] = features[parity * 64 : parity * 64 + 64]


def spread(zh, turned, far):
    return pl.pallas_call(
        spread_kernel,
        in_specs=[SMEM] + [VMEM] * 2,
        out_specs=VMEM,
        out_shape=jax.ShapeDtypeStruct((8, 2, 64, 384), jnp.bfloat16),
        compiler_params=PARAMS,
        name="spread",
    )(zh[None], turned, far)


def stack_kernel(parity_ref, own_ref, other_ref, out_ref, sems):
    parity = parity_ref[0]
    copies = [
        pltpu.make_async_copy(
            source, out_ref.at[pl.ds(pl.multiple_of(place * 384, 384), 384)], sems.at[i]
        )
        for i, (source, place) in enumerate(((own_ref, parity), (other_ref, 1 - parity)))
    ]
    for copy in copies:
        copy.start()
    for copy in copies:
        copy.wait()


def stack(parity, own, other):
    return pl.pallas_call(
        stack_kernel,
        in_specs=[SMEM] + [pl.BlockSpec(memory_space=pl.ANY)] * 2,
        out_specs=VMEM,
        out_shape=jax.ShapeDtypeStruct((768, 2 * BLK), jnp.bfloat16),
        scratch_shapes=[pltpu.SemaphoreType.DMA((2,))],
        compiler_params=PARAMS,
        cost_estimate=EARLY,
        name="stack",
    )(parity[None], own, other)


def contract_kernel(half_ref, features_ref, cotangent_ref, out_ref):
    rows = pl.ds(pl.multiple_of(half_ref[0] * ROWS, ROWS), ROWS)
    features = jnp.concatenate(
        [
            jnp.concatenate(
                [features_ref[parity, :, zh, rows, :].reshape(128, 384) for zh in range(2)], axis=0
            )
            for parity in range(2)
        ],
        axis=1,
    )
    out_ref[...] = dot(features, cotangent_ref[...]).astype(out_ref.dtype)


def contract(half, features, cotangent, dtype):
    return pl.pallas_call(
        contract_kernel,
        in_specs=[SMEM] + [VMEM] * 2,
        out_specs=VMEM,
        out_shape=jax.ShapeDtypeStruct((256, 2 * BLK), dtype),
        compiler_params=PARAMS,
        name="contract",
    )(half[None], features, cotangent)


def add_kernel(keep_ref, arrived_ref, shares_ref):
    for place in range(8):
        rows = slice(place * ROWS, place * ROWS + ROWS)
        total = (keep_ref[rows] + arrived_ref[rows].astype(jnp.float32)).astype(jnp.bfloat16)
        shares_ref[place * 2] = total[:, :BLK]
        shares_ref[place * 2 + 1] = total[:, BLK:]


def add(keep, arrived):
    return pl.pallas_call(
        add_kernel,
        in_specs=[VMEM] * 2,
        out_specs=VMEM,
        out_shape=jax.ShapeDtypeStruct((16, ROWS, BLK), jnp.bfloat16),
        compiler_params=PARAMS,
        name="add",
    )(keep, arrived)


def total_kernel(shares_ref, copies_ref):
    total = shares_ref[0].astype(jnp.float32)
    for share in range(1, 16):
        total += shares_ref[share].astype(jnp.float32)
    total = total.astype(jnp.bfloat16)
    for copy in range(8):
        copies_ref[copy] = total


def total_copies(shares):
    return pl.pallas_call(
        total_kernel,
        in_specs=[VMEM],
        out_specs=VMEM,
        out_shape=jax.ShapeDtypeStruct((8, ROWS, BLK), jnp.bfloat16),
        compiler_params=PARAMS,
        name="total_copies",
    )(shares)


def symmetric_product(left, right, store, rows=None):
    top = left[:HALF, :] if rows is None else jnp.concatenate([left[:HALF, :], rows], axis=0)
    top = dot(top, right[...])
    store(0, 0, top[:HALF, :HALF])
    store(0, HALF, top[:HALF, HALF:])
    store(HALF, HALF, dot(left[HALF:, :], right[:, HALF:]))
    return top[HALF:].astype(jnp.bfloat16)


def put(ref, i, j, value):
    ref[i : i + HALF, j : j + HALF] = value
    if i != j:
        ref[j : j + HALF, i : i + HALF] = value.T


def rounded(ref):
    return lambda i, j, value: put(ref, i, j, value.astype(jnp.bfloat16))


def roots_kernel(
    place_ref, block_ref, out_ref, flipped_ref, *scratch
):
    lgram, rgram, lstep, rstep, lsquare, rsquare, lfourth, rfourth, lmat, rmat, rroot = scratch
    flipped_ref[...] = block_ref[...].T
    wide = block_ref[...].astype(jnp.float32)
    trace = jnp.sum(wide * wide, keepdims=True)
    damp = 0.1 * trace / BLK + 1e-06
    diagonal = lax.broadcasted_iota(jnp.int32, (HALF, HALF), 0) == lax.broadcasted_iota(
        jnp.int32, (HALF, HALF), 1
    )
    base = jnp.where(diagonal, 1.25, 0.0)

    def set_step(step, i, j, value):
        put(step, i, j, ((base if i == j else 0.0) - value * 0.25).astype(jnp.bfloat16))

    def start(left, right, gram, mat, step):
        parts = []

        def store(i, j, value):
            gram[i : i + HALF, j : j + HALF] = value
            if i == j:
                value = value + jnp.where(diagonal, damp, 0.0)
            parts.append(jnp.sum(value * value, keepdims=True) * (1.0 if i == j else 2.0))

        symmetric_product(left, right, store)
        inverse = lax.rsqrt(parts[0] + parts[1] + parts[2])
        for i, j in ((0, 0), (0, HALF), (HALF, HALF)):
            value = gram[i : i + HALF, j : j + HALF]
            if i == j:
                value = value + jnp.where(diagonal, damp, 0.0)
            value = value * inverse
            put(mat, i, j, value.astype(jnp.bfloat16))
            set_step(step, i, j, value)
        return jnp.sqrt(jnp.sqrt(inverse))

    lscale = start(block_ref, flipped_ref, lgram, lmat, lstep)
    rscale = start(flipped_ref, block_ref, rgram, rmat, rstep)
    ids = lax.broadcasted_iota(jnp.int32, (ROWS, BLK), 0)
    picked = jnp.where(ids < 16, ids + place_ref[0], ids - 16 + place_ref[1])
    columns = lax.broadcasted_iota(jnp.int32, (ROWS, BLK), 1)
    rows = jnp.where(columns == picked, lscale, 0.0).astype(jnp.bfloat16)
    rroot[...] = rstep[...] * rscale.astype(jnp.bfloat16)
    for it in range(ITERS - 1):
        rows = symmetric_product(lstep, lstep, rounded(lsquare), rows)
        symmetric_product(rstep, rstep, rounded(rsquare))
        if it > 0:
            rroot[...] = dot(rroot[...], rstep[...]).astype(jnp.bfloat16)
        symmetric_product(lsquare, lsquare, rounded(lfourth))
        symmetric_product(rsquare, rsquare, rounded(rfourth))
        for fourth, mat, step in ((lfourth, lmat, lstep), (rfourth, rmat, rstep)):
            parts = []
            symmetric_product(fourth, mat, lambda i, j, value: parts.append((i, j, value)))
            for i, j, value in parts:
                if it < ITERS - 2:
                    put(mat, i, j, value.astype(jnp.bfloat16))
                set_step(step, i, j, value)
    rows = dot(rows, lstep[...]).astype(jnp.bfloat16)
    half = dot(rows, block_ref[...]).astype(jnp.bfloat16)
    rroot[...] = dot(rroot[...], rstep[...]).astype(jnp.bfloat16)
    value = dot(half, rroot[...]).astype(jnp.bfloat16)
    out_ref[...] = value


def apply_roots(places, block):
    piece = jax.ShapeDtypeStruct((ROWS, BLK), jnp.bfloat16)
    narrow = pltpu.VMEM((BLK, BLK), jnp.bfloat16)
    return pl.pallas_call(
        roots_kernel,
        in_specs=[SMEM, VMEM],
        out_specs=VMEM,
        out_shape=piece,
        scratch_shapes=[narrow] + [pltpu.VMEM((BLK, BLK), jnp.float32)] * 2 + [narrow] * 9,
        compiler_params=PARAMS,
        name="apply_roots",
    )(places, block)


def join_kernel(zp_ref, pieces_ref, out_ref):
    rows = pl.ds(pl.multiple_of(zp_ref[0] * 16, 16), 16)
    for column in range(2):
        out_ref[:, column * BLK : column * BLK + BLK] = pieces_ref[column, rows, :]


def join(zp, pieces):
    return pl.pallas_call(
        join_kernel,
        in_specs=[SMEM, VMEM],
        out_specs=VMEM,
        out_shape=jax.ShapeDtypeStruct((16, 2 * BLK), jnp.bfloat16),
        compiler_params=PARAMS,
        name="join",
    )(zp[None], pieces)


def swap(value, axis):
    return lax.ppermute(value, axis, [(0, 1), (1, 0)])


def exchange(value, axes):
    return lax.all_to_all(value, axes, 0, 0, tiled=True)


def partner(y, core):
    return (y + 1 if (y + core) % 2 == 0 else y - 1) % 8


def pair_groups():
    groups = []
    for core in range(2):
        for even in range(0, 8, 2):
            pair = (even, partner(even, core))
            for zh in range(2):
                groups.append(
                    [(y * 2 + core) * 8 + zh * 4 + x for y in pair for x in range(4)]
                )
    return groups


def body(tokens, cotangent):
    core, p, q, zp = (lax.axis_index(name) for name in ("core", "p", "q", "zp"))
    pairs = [(y * 2 + k, partner(y, k) * 2 + k) for y in range(8) for k in range(2)]
    other = lax.ppermute(cotangent, ("q", "p", "core"), pairs)
    features = lax.all_to_all(
        spread(lax.axis_index("zh"), turn(tokens), swap(tokens, "zh")),
        ("q", "p", "core", "zh", "x"),
        0,
        0,
        axis_index_groups=pair_groups(),
        tiled=True,
    ).reshape(2, 4, 2, 64, 384)
    both = stack(p, cotangent, other)
    place = p * 256 + ((q & 1) * 4 + (q >> 1)) * ROWS + core * 16
    places = jnp.stack([place, place + 64])
    arrived = swap(contract(1 - core, features, both, jnp.bfloat16), "core")
    keep = contract(core, features, both, jnp.float32)
    arrived, places, zp = lax.optimization_barrier((arrived, places, zp))
    shares = exchange(add(keep, arrived), ("zr", "q", "zp"))
    own = exchange(total_copies(shares), ("p", "q")).reshape(256, BLK)
    update = apply_roots(places, lax.all_gather(own, "core", axis=0, tiled=True))
    return join(zp, lax.all_gather(update[None], "zp", axis=0, tiled=True))


def solution(mesh):
    devices = mesh.devices.reshape(2, 2, 4, 2, 2, 2, 4)
    fine = Mesh(devices, ("zr", "zp", "q", "p", "core", "zh", "x"))
    spec = P(("zr", "zp", "q", "p", "core"), ("zh", "x"))
    return jax.shard_map(
        body, mesh=fine, in_specs=(spec, spec), out_specs=spec, check_vma=False
    )
```

```python
import jax
import jax.numpy as jnp
from jax import lax
from jax.experimental import pallas as pl
from jax.experimental.pallas import tpu as pltpu
from jax.sharding import Mesh
from jax.sharding import PartitionSpec as P

BLK = 512
HALF = 256
ITERS = 4
ROWS = 32
ORDER = (0, 2, 1, 3)
PARAMS = pltpu.CompilerParams(vmem_limit_bytes=24 * 1024 * 1024)
VMEM = pl.BlockSpec(memory_space=pltpu.VMEM)
SMEM = pl.BlockSpec(memory_space=pltpu.SMEM)
EARLY = pl.CostEstimate(flops=7 * 10**9, bytes_accessed=3 << 20, transcendentals=0)


def dot(left, right):
    return jnp.dot(left, right, preferred_element_type=jnp.float32)


def turn_kernel(tokens_ref, turned_ref):
    turned_ref[...] = tokens_ref[...].T


def turn(tokens):
    return pl.pallas_call(
        turn_kernel,
        in_specs=[VMEM],
        out_specs=VMEM,
        out_shape=jax.ShapeDtypeStruct((128, 384), jnp.bfloat16),
        compiler_params=PARAMS,
        name="turn",
    )(tokens)


def spread_kernel(zh_ref, turned_ref, far_ref, copies_ref):
    zh = zh_ref[0]
    for features, at in ((turned_ref[...], zh), (far_ref[...].T, 1 - zh)):
        for parity in range(2):
            for place in range(4):
                copies_ref[parity * 4 + place, at] = features[parity * 64 : parity * 64 + 64]


def spread(zh, turned, far):
    return pl.pallas_call(
        spread_kernel,
        in_specs=[SMEM] + [VMEM] * 2,
        out_specs=VMEM,
        out_shape=jax.ShapeDtypeStruct((8, 2, 64, 384), jnp.bfloat16),
        compiler_params=PARAMS,
        name="spread",
    )(zh[None], turned, far)


def stack_kernel(parity_ref, own_ref, other_ref, out_ref, sems):
    parity = parity_ref[0]
    copies = [
        pltpu.make_async_copy(
            source, out_ref.at[pl.ds(pl.multiple_of(place * 384, 384), 384)], sems.at[i]
        )
        for i, (source, place) in enumerate(((own_ref, parity), (other_ref, 1 - parity)))
    ]
    for copy in copies:
        copy.start()
    for copy in copies:
        copy.wait()


def stack(parity, own, other):
    return pl.pallas_call(
        stack_kernel,
        in_specs=[SMEM] + [pl.BlockSpec(memory_space=pl.ANY)] * 2,
        out_specs=VMEM,
        out_shape=jax.ShapeDtypeStruct((768, 2 * BLK), jnp.bfloat16),
        scratch_shapes=[pltpu.SemaphoreType.DMA((2,))],
        compiler_params=PARAMS,
        cost_estimate=EARLY,
        name="stack",
    )(parity[None], own, other)


def contract_kernel(half_ref, features_ref, cotangent_ref, out_ref):
    rows = pl.ds(pl.multiple_of(half_ref[0] * ROWS, ROWS), ROWS)
    features = jnp.concatenate(
        [
            jnp.concatenate(
                [features_ref[parity, :, zh, rows, :].reshape(128, 384) for zh in range(2)], axis=0
            )
            for parity in range(2)
        ],
        axis=1,
    )
    out_ref[...] = dot(features, cotangent_ref[...]).astype(out_ref.dtype)


def contract(half, features, cotangent, dtype):
    return pl.pallas_call(
        contract_kernel,
        in_specs=[SMEM] + [VMEM] * 2,
        out_specs=VMEM,
        out_shape=jax.ShapeDtypeStruct((256, 2 * BLK), dtype),
        compiler_params=PARAMS,
        name="contract",
    )(half[None], features, cotangent)


def add_kernel(keep_ref, arrived_ref, shares_ref):
    for place in range(8):
        rows = slice(place * ROWS, place * ROWS + ROWS)
        total = (keep_ref[rows] + arrived_ref[rows].astype(jnp.float32)).astype(jnp.bfloat16)
        share = (place // 4 * 4 + ORDER.index(place % 4)) * 2
        shares_ref[share] = total[:, :BLK]
        shares_ref[share + 1] = total[:, BLK:]


def add(keep, arrived):
    return pl.pallas_call(
        add_kernel,
        in_specs=[VMEM] * 2,
        out_specs=VMEM,
        out_shape=jax.ShapeDtypeStruct((16, ROWS, BLK), jnp.bfloat16),
        compiler_params=PARAMS,
        name="add",
    )(keep, arrived)


def total_kernel(shares_ref, copies_ref):
    total = shares_ref[0].astype(jnp.float32)
    for share in range(1, 16):
        total += shares_ref[share].astype(jnp.float32)
    total = total.astype(jnp.bfloat16)
    for copy in range(8):
        copies_ref[copy] = total


def total_copies(shares):
    return pl.pallas_call(
        total_kernel,
        in_specs=[VMEM],
        out_specs=VMEM,
        out_shape=jax.ShapeDtypeStruct((8, ROWS, BLK), jnp.bfloat16),
        compiler_params=PARAMS,
        name="total_copies",
    )(shares)


def symmetric_product(left, right, store, rows=None):
    top = left[:HALF, :] if rows is None else jnp.concatenate([left[:HALF, :], rows], axis=0)
    top = dot(top, right[...])
    store(0, 0, top[:HALF, :HALF])
    store(0, HALF, top[:HALF, HALF:])
    store(HALF, HALF, dot(left[HALF:, :], right[:, HALF:]))
    return top[HALF:].astype(jnp.bfloat16)


def put(ref, i, j, value):
    ref[i : i + HALF, j : j + HALF] = value
    if i != j:
        ref[j : j + HALF, i : i + HALF] = value.T


def rounded(ref):
    return lambda i, j, value: put(ref, i, j, value.astype(jnp.bfloat16))


def roots_kernel(
    place_ref, block_ref, out_ref, flipped_ref, *scratch
):
    lgram, rgram, lstep, rstep, lsquare, rsquare, lfourth, rfourth, lmat, rmat, rroot = scratch
    flipped_ref[...] = block_ref[...].T
    wide = block_ref[...].astype(jnp.float32)
    trace = jnp.sum(wide * wide, keepdims=True)
    damp = 0.1 * trace / BLK + 1e-06
    diagonal = lax.broadcasted_iota(jnp.int32, (HALF, HALF), 0) == lax.broadcasted_iota(
        jnp.int32, (HALF, HALF), 1
    )
    base = jnp.where(diagonal, 1.25, 0.0)

    def set_step(step, i, j, value):
        put(step, i, j, ((base if i == j else 0.0) - value * 0.25).astype(jnp.bfloat16))

    def start(left, right, gram, mat, step):
        parts = []

        def store(i, j, value):
            gram[i : i + HALF, j : j + HALF] = value
            if i == j:
                value = value + jnp.where(diagonal, damp, 0.0)
            parts.append(jnp.sum(value * value, keepdims=True) * (1.0 if i == j else 2.0))

        symmetric_product(left, right, store)
        inverse = lax.rsqrt(parts[0] + parts[1] + parts[2])
        for i, j in ((0, 0), (0, HALF), (HALF, HALF)):
            value = gram[i : i + HALF, j : j + HALF]
            if i == j:
                value = value + jnp.where(diagonal, damp, 0.0)
            value = value * inverse
            put(mat, i, j, value.astype(jnp.bfloat16))
            set_step(step, i, j, value)
        return jnp.sqrt(jnp.sqrt(inverse))

    lscale = start(block_ref, flipped_ref, lgram, lmat, lstep)
    rscale = start(flipped_ref, block_ref, rgram, rmat, rstep)
    ids = lax.broadcasted_iota(jnp.int32, (ROWS, BLK), 0)
    picked = jnp.where(ids < 16, ids + place_ref[0], ids - 16 + place_ref[1])
    columns = lax.broadcasted_iota(jnp.int32, (ROWS, BLK), 1)
    rows = jnp.where(columns == picked, lscale, 0.0).astype(jnp.bfloat16)
    rroot[...] = rstep[...] * rscale.astype(jnp.bfloat16)
    for it in range(ITERS - 1):
        rows = symmetric_product(lstep, lstep, rounded(lsquare), rows)
        symmetric_product(rstep, rstep, rounded(rsquare))
        if it > 0:
            rroot[...] = dot(rroot[...], rstep[...]).astype(jnp.bfloat16)
        symmetric_product(lsquare, lsquare, rounded(lfourth))
        symmetric_product(rsquare, rsquare, rounded(rfourth))
        for fourth, mat, step in ((lfourth, lmat, lstep), (rfourth, rmat, rstep)):
            parts = []
            symmetric_product(fourth, mat, lambda i, j, value: parts.append((i, j, value)))
            for i, j, value in parts:
                if it < ITERS - 2:
                    put(mat, i, j, value.astype(jnp.bfloat16))
                set_step(step, i, j, value)
    rows = dot(rows, lstep[...]).astype(jnp.bfloat16)
    half = dot(rows, block_ref[...]).astype(jnp.bfloat16)
    rroot[...] = dot(rroot[...], rstep[...]).astype(jnp.bfloat16)
    value = dot(half, rroot[...]).astype(jnp.bfloat16)
    out_ref[...] = value


def apply_roots(places, block):
    piece = jax.ShapeDtypeStruct((ROWS, BLK), jnp.bfloat16)
    narrow = pltpu.VMEM((BLK, BLK), jnp.bfloat16)
    return pl.pallas_call(
        roots_kernel,
        in_specs=[SMEM, VMEM],
        out_specs=VMEM,
        out_shape=piece,
        scratch_shapes=[narrow] + [pltpu.VMEM((BLK, BLK), jnp.float32)] * 2 + [narrow] * 9,
        compiler_params=PARAMS,
        name="apply_roots",
    )(places, block)


def join_kernel(zp_ref, pieces_ref, out_ref):
    rows = pl.ds(pl.multiple_of(zp_ref[0] * 16, 16), 16)
    for column in range(2):
        out_ref[:, column * BLK : column * BLK + BLK] = pieces_ref[column, rows, :]


def join(zp, pieces):
    return pl.pallas_call(
        join_kernel,
        in_specs=[SMEM, VMEM],
        out_specs=VMEM,
        out_shape=jax.ShapeDtypeStruct((16, 2 * BLK), jnp.bfloat16),
        compiler_params=PARAMS,
        name="join",
    )(zp[None], pieces)


def swap(value, axis):
    return lax.ppermute(value, axis, [(0, 1), (1, 0)])


def exchange(value, axes, groups):
    return lax.all_to_all(value, axes, 0, 0, axis_index_groups=groups, tiled=True)


def partner(y, core):
    return (y + 1 if (y + core) % 2 == 0 else y - 1) % 8


def pair_groups():
    groups = []
    for core in range(2):
        for even in range(0, 8, 2):
            pair = (even, partner(even, core))
            for zh in range(2):
                groups.append(
                    [(y * 2 + core) * 8 + zh * 4 + x for y in pair for x in range(4)]
                )
    return groups


def body(tokens, cotangent):
    core, p, q, zp = (lax.axis_index(name) for name in ("core", "p", "q", "zp"))
    pairs = [(y * 2 + k, partner(y, k) * 2 + k) for y in range(8) for k in range(2)]
    other = lax.ppermute(cotangent, ("q", "p", "core"), pairs)
    features = exchange(
        spread(lax.axis_index("zh"), turn(tokens), swap(tokens, "zh")),
        ("q", "p", "core", "zh", "x"),
        pair_groups(),
    ).reshape(2, 4, 2, 64, 384)
    both = stack(p, cotangent, other)
    place = p * 256 + ((q & 1) * 4 + (q >> 1) * 2) * ROWS + core * 16
    places = jnp.stack([place, place + ROWS])
    arrived = swap(contract(1 - core, features, both, jnp.bfloat16), "core")
    keep = contract(core, features, both, jnp.float32)
    arrived, places, zp = lax.optimization_barrier((arrived, places, zp))
    chips = [zr * 8 + zp * 4 + q for zr in range(2) for q in ORDER for zp in range(2)]
    shares = exchange(add(keep, arrived), ("zr", "zp", "q"), [chips])
    ring = [q * 2 + p for p in range(2) for q in ORDER]
    own = exchange(total_copies(shares), ("q", "p"), [ring]).reshape(256, BLK)
    update = apply_roots(places, lax.all_gather(own, "core", axis=0, tiled=True))
    return join(zp, lax.all_gather(update[None], "zp", axis=0, tiled=True))


def solution(mesh):
    devices = mesh.devices.reshape(2, 2, 4, 2, 2, 2, 4)
    fine = Mesh(devices, ("zr", "zp", "q", "p", "core", "zh", "x"))
    spec = P(("zr", "zp", "q", "p", "core"), ("zh", "x"))
    return jax.shard_map(
        body, mesh=fine, in_specs=(spec, spec), out_specs=spec, check_vma=False
    )
```

```python
import jax
import jax.numpy as jnp
from jax import lax
from jax.experimental import pallas as pl
from jax.experimental.pallas import tpu as pltpu
from jax.sharding import Mesh
from jax.sharding import PartitionSpec as P

BLK = 512
HALF = 256
ITERS = 4
ROWS = 32
ORDER = (0, 2, 1, 3)
XS = ((0, 1, 2, 3), (2, 3, 0, 1))
PARAMS = pltpu.CompilerParams(vmem_limit_bytes=24 * 1024 * 1024)
VMEM = pl.BlockSpec(memory_space=pltpu.VMEM)
SMEM = pl.BlockSpec(memory_space=pltpu.SMEM)
EARLY = pl.CostEstimate(flops=7 * 10**9, bytes_accessed=3 << 20, transcendentals=0)


def dot(left, right):
    return jnp.dot(left, right, preferred_element_type=jnp.float32)


def turn_kernel(tokens_ref, turned_ref):
    turned_ref[...] = tokens_ref[...].T


def turn(tokens):
    return pl.pallas_call(
        turn_kernel,
        in_specs=[VMEM],
        out_specs=VMEM,
        out_shape=jax.ShapeDtypeStruct((128, 384), jnp.bfloat16),
        compiler_params=PARAMS,
        name="turn",
    )(tokens)


def spread_kernel(zh_ref, turned_ref, far_ref, copies_ref):
    zh = zh_ref[0]
    for features, at in ((turned_ref[...], zh), (far_ref[...].T, 1 - zh)):
        for parity in range(2):
            for place in range(4):
                copies_ref[parity * 4 + place, at] = features[parity * 64 : parity * 64 + 64]


def spread(zh, turned, far):
    return pl.pallas_call(
        spread_kernel,
        in_specs=[SMEM] + [VMEM] * 2,
        out_specs=VMEM,
        out_shape=jax.ShapeDtypeStruct((8, 2, 64, 384), jnp.bfloat16),
        compiler_params=PARAMS,
        name="spread",
    )(zh[None], turned, far)


def stack_kernel(parity_ref, own_ref, other_ref, out_ref, sems):
    parity = parity_ref[0]
    copies = [
        pltpu.make_async_copy(
            source, out_ref.at[pl.ds(pl.multiple_of(place * 384, 384), 384)], sems.at[i]
        )
        for i, (source, place) in enumerate(((own_ref, parity), (other_ref, 1 - parity)))
    ]
    for copy in copies:
        copy.start()
    for copy in copies:
        copy.wait()


def stack(parity, own, other):
    return pl.pallas_call(
        stack_kernel,
        in_specs=[SMEM] + [pl.BlockSpec(memory_space=pl.ANY)] * 2,
        out_specs=VMEM,
        out_shape=jax.ShapeDtypeStruct((768, 2 * BLK), jnp.bfloat16),
        scratch_shapes=[pltpu.SemaphoreType.DMA((2,))],
        compiler_params=PARAMS,
        cost_estimate=EARLY,
        name="stack",
    )(parity[None], own, other)


def contract_kernel(half_ref, features_ref, cotangent_ref, out_ref):
    rows = pl.ds(pl.multiple_of(half_ref[0] * ROWS, ROWS), ROWS)
    features = jnp.concatenate(
        [
            jnp.concatenate(
                [
                    features_ref[parity, XS[parity].index(x), zh, rows, :]
                    for zh in range(2)
                    for x in range(4)
                ],
                axis=0,
            )
            for parity in range(2)
        ],
        axis=1,
    )
    out_ref[...] = dot(features, cotangent_ref[...]).astype(out_ref.dtype)


def contract(half, features, cotangent, dtype):
    return pl.pallas_call(
        contract_kernel,
        in_specs=[SMEM] + [VMEM] * 2,
        out_specs=VMEM,
        out_shape=jax.ShapeDtypeStruct((256, 2 * BLK), dtype),
        compiler_params=PARAMS,
        name="contract",
    )(half[None], features, cotangent)


def add_kernel(keep_ref, arrived_ref, shares_ref):
    for place in range(8):
        rows = slice(place * ROWS, place * ROWS + ROWS)
        total = (keep_ref[rows] + arrived_ref[rows].astype(jnp.float32)).astype(jnp.bfloat16)
        share = (place // 4 * 4 + ORDER.index(place % 4)) * 2
        shares_ref[share] = total[:, :BLK]
        shares_ref[share + 1] = total[:, BLK:]


def add(keep, arrived):
    return pl.pallas_call(
        add_kernel,
        in_specs=[VMEM] * 2,
        out_specs=VMEM,
        out_shape=jax.ShapeDtypeStruct((16, ROWS, BLK), jnp.bfloat16),
        compiler_params=PARAMS,
        name="add",
    )(keep, arrived)


def total_kernel(shares_ref, copies_ref):
    total = shares_ref[0].astype(jnp.float32)
    for share in range(1, 16):
        total += shares_ref[share].astype(jnp.float32)
    total = total.astype(jnp.bfloat16)
    for copy in range(8):
        copies_ref[copy] = total


def total_copies(shares):
    return pl.pallas_call(
        total_kernel,
        in_specs=[VMEM],
        out_specs=VMEM,
        out_shape=jax.ShapeDtypeStruct((8, ROWS, BLK), jnp.bfloat16),
        compiler_params=PARAMS,
        name="total_copies",
    )(shares)


def symmetric_product(left, right, store, rows=None):
    top = left[:HALF, :] if rows is None else jnp.concatenate([left[:HALF, :], rows], axis=0)
    top = dot(top, right[...])
    store(0, 0, top[:HALF, :HALF])
    store(0, HALF, top[:HALF, HALF:])
    store(HALF, HALF, dot(left[HALF:, :], right[:, HALF:]))
    return top[HALF:].astype(jnp.bfloat16)


def put(ref, i, j, value):
    ref[i : i + HALF, j : j + HALF] = value
    if i != j:
        ref[j : j + HALF, i : i + HALF] = value.T


def rounded(ref):
    return lambda i, j, value: put(ref, i, j, value.astype(jnp.bfloat16))


def roots_kernel(
    place_ref, block_ref, out_ref, flipped_ref, *scratch
):
    lgram, rgram, lstep, rstep, lsquare, rsquare, lfourth, rfourth, lmat, rmat, rroot = scratch
    flipped_ref[...] = block_ref[...].T
    wide = block_ref[...].astype(jnp.float32)
    trace = jnp.sum(wide * wide, keepdims=True)
    damp = 0.1 * trace / BLK + 1e-06
    diagonal = lax.broadcasted_iota(jnp.int32, (HALF, HALF), 0) == lax.broadcasted_iota(
        jnp.int32, (HALF, HALF), 1
    )
    base = jnp.where(diagonal, 1.25, 0.0)

    def set_step(step, i, j, value):
        put(step, i, j, ((base if i == j else 0.0) - value * 0.25).astype(jnp.bfloat16))

    def start(left, right, gram, mat, step):
        parts = []

        def store(i, j, value):
            gram[i : i + HALF, j : j + HALF] = value
            if i == j:
                value = value + jnp.where(diagonal, damp, 0.0)
            parts.append(jnp.sum(value * value, keepdims=True) * (1.0 if i == j else 2.0))

        symmetric_product(left, right, store)
        inverse = lax.rsqrt(parts[0] + parts[1] + parts[2])
        for i, j in ((0, 0), (0, HALF), (HALF, HALF)):
            value = gram[i : i + HALF, j : j + HALF]
            if i == j:
                value = value + jnp.where(diagonal, damp, 0.0)
            value = value * inverse
            put(mat, i, j, value.astype(jnp.bfloat16))
            set_step(step, i, j, value)
        return jnp.sqrt(jnp.sqrt(inverse))

    lscale = start(block_ref, flipped_ref, lgram, lmat, lstep)
    rscale = start(flipped_ref, block_ref, rgram, rmat, rstep)
    ids = lax.broadcasted_iota(jnp.int32, (ROWS, BLK), 0)
    picked = jnp.where(ids < 16, ids + place_ref[0], ids - 16 + place_ref[1])
    columns = lax.broadcasted_iota(jnp.int32, (ROWS, BLK), 1)
    rows = jnp.where(columns == picked, lscale, 0.0).astype(jnp.bfloat16)
    rroot[...] = rstep[...] * rscale.astype(jnp.bfloat16)
    for it in range(ITERS - 1):
        rows = symmetric_product(lstep, lstep, rounded(lsquare), rows)
        symmetric_product(rstep, rstep, rounded(rsquare))
        if it > 0:
            rroot[...] = dot(rroot[...], rstep[...]).astype(jnp.bfloat16)
        symmetric_product(lsquare, lsquare, rounded(lfourth))
        symmetric_product(rsquare, rsquare, rounded(rfourth))
        for fourth, mat, step in ((lfourth, lmat, lstep), (rfourth, rmat, rstep)):
            parts = []
            symmetric_product(fourth, mat, lambda i, j, value: parts.append((i, j, value)))
            for i, j, value in parts:
                if it < ITERS - 2:
                    put(mat, i, j, value.astype(jnp.bfloat16))
                set_step(step, i, j, value)
    rows = dot(rows, lstep[...]).astype(jnp.bfloat16)
    half = dot(rows, block_ref[...]).astype(jnp.bfloat16)
    rroot[...] = dot(rroot[...], rstep[...]).astype(jnp.bfloat16)
    value = dot(half, rroot[...]).astype(jnp.bfloat16)
    out_ref[...] = value


def apply_roots(places, block):
    piece = jax.ShapeDtypeStruct((ROWS, BLK), jnp.bfloat16)
    narrow = pltpu.VMEM((BLK, BLK), jnp.bfloat16)
    return pl.pallas_call(
        roots_kernel,
        in_specs=[SMEM, VMEM],
        out_specs=VMEM,
        out_shape=piece,
        scratch_shapes=[narrow] + [pltpu.VMEM((BLK, BLK), jnp.float32)] * 2 + [narrow] * 9,
        compiler_params=PARAMS,
        name="apply_roots",
    )(places, block)


def join_kernel(zp_ref, pieces_ref, out_ref):
    rows = pl.ds(pl.multiple_of(zp_ref[0] * 16, 16), 16)
    for column in range(2):
        out_ref[:, column * BLK : column * BLK + BLK] = pieces_ref[column, rows, :]


def join(zp, pieces):
    return pl.pallas_call(
        join_kernel,
        in_specs=[SMEM, VMEM],
        out_specs=VMEM,
        out_shape=jax.ShapeDtypeStruct((16, 2 * BLK), jnp.bfloat16),
        compiler_params=PARAMS,
        name="join",
    )(zp[None], pieces)


def swap(value, axis):
    return lax.ppermute(value, axis, [(0, 1), (1, 0)])


def exchange(value, axes, groups):
    return lax.all_to_all(value, axes, 0, 0, axis_index_groups=groups, tiled=True)


def partner(y, core):
    return (y + 1 if (y + core) % 2 == 0 else y - 1) % 8


def pair_groups():
    groups = []
    for core in range(2):
        for even in range(0, 8, 2):
            pair = (even, partner(even, core))
            for zh in range(2):
                groups.append(
                    [(y * 2 + core) * 8 + zh * 4 + x for y, xs in zip(pair, XS) for x in xs]
                )
    return groups


def body(tokens, cotangent):
    core, p, q, zp = (lax.axis_index(name) for name in ("core", "p", "q", "zp"))
    pairs = [(y * 2 + k, partner(y, k) * 2 + k) for y in range(8) for k in range(2)]
    other = lax.ppermute(cotangent, ("q", "p", "core"), pairs)
    features = exchange(
        spread(lax.axis_index("zh"), turn(tokens), swap(tokens, "zh")),
        ("q", "p", "core", "zh", "x"),
        pair_groups(),
    ).reshape(2, 4, 2, 64, 384)
    both = stack(p, cotangent, other)
    place = p * 256 + ((q & 1) * 4 + (q >> 1) * 2) * ROWS + core * 16
    places = jnp.stack([place, place + ROWS])
    arrived = swap(contract(1 - core, features, both, jnp.bfloat16), "core")
    keep = contract(core, features, both, jnp.float32)
    arrived, places, zp = lax.optimization_barrier((arrived, places, zp))
    chips = [zr * 8 + zp * 4 + q for zr in range(2) for q in ORDER for zp in range(2)]
    shares = exchange(add(keep, arrived), ("zr", "zp", "q"), [chips])
    ring = [q * 2 + p for p in range(2) for q in ORDER]
    own = exchange(total_copies(shares), ("q", "p"), [ring]).reshape(256, BLK)
    update = apply_roots(places, lax.all_gather(own, "core", axis=0, tiled=True))
    return join(zp, lax.all_gather(update[None], "zp", axis=0, tiled=True))


def solution(mesh):
    devices = mesh.devices.reshape(2, 2, 4, 2, 2, 2, 4)
    fine = Mesh(devices, ("zr", "zp", "q", "p", "core", "zh", "x"))
    spec = P(("zr", "zp", "q", "p", "core"), ("zh", "x"))
    return jax.shard_map(
        body, mesh=fine, in_specs=(spec, spec), out_specs=spec, check_vma=False
    )
```
